32 devices in a mesh: prod: 4 (over y, x), cand: 8 (over z, core).
Axes of the slice: x: 2, y: 2, z: 4, core: 2. Of those that a mesh axis runs over, the one named last changes fastest.
Arguments:
- cand_states: bfloat16 [4, 8, 128, 4096], P('prod', 'cand'), may hold values from -600 to 600
- enc_rows: bfloat16 [4, 256, 4096], P('prod', 'cand'), may hold values from -120 to 120
- w_query: bfloat16 [4096, 4096], P('prod', 'cand'), may hold values from -0.09375 to 0.09375
- w_key: bfloat16 [4096, 4096], P('prod', 'cand'), may hold values from -0.09375 to 0.09375
- w_value: bfloat16 [4096, 4096], P('prod', 'cand'), may hold values from -0.09375 to 0.09375
- w_out: bfloat16 [4096, 4096], P('cand', 'prod'), may hold values from -0.375 to 0.375
- tile_mask: int32 [4, 8, 2], P('prod', 'cand'), may hold values from 0 to 1, as said below
- counts: int32 [4], P('prod'), may hold values from 1 to 8, as said below
Outputs:
- cross_out: bfloat16 [4, 8, 128, 4096], P('prod', 'cand')
The draws below stay inside these ranges and needn't reach their ends.
Inputs may be any that keep to these rules, and one draw needn't show every extreme that they name: `tile_mask`: every candidate has at least one tile set. `counts`: some product fills all 8 slots.
All inputs are finite; a program needn't handle non-finite values.
Results may differ from the reference program's by a relative error of at most 0.023.
The reference program's roundings to bfloat16 on the way count: a program that leaves them out, or rounds other values in their place, can miss the bound.
Values may be sent and summed in bfloat16 or wider, within the bound.
No kernel may reach another device: no remote copies, remote signals or barrier semaphores. Data moves between devices by JAX's collectives and lax.ppermute only.
A program may use at most 128 MiB of HBM per device.

```python
import math
import jax
import jax.numpy as jnp
from jax import lax

D = 4096
HEADS = 64
HD = 64
CLEN = 128
ELEN = 256
TILE = 128
ETILES = 2
PRODUCTS = 4
CANDS = 8
GROUP = 512
N_CAND = 8


def draw_cand_states(key, part):
    first, second, third = jax.random.split(key, 3)
    shape = (PRODUCTS, CANDS, CLEN, D)
    row_scale = jnp.exp(jax.random.uniform(first, (PRODUCTS, CANDS, CLEN, 1), jnp.float32, 0.0, math.log(10.0)))
    col_scale = jnp.exp(jax.random.uniform(second, (D,), jnp.float32, 0.0, math.log(10.0)))
    base = jnp.clip(jax.random.normal(third, shape, jnp.float32), -4.0, 4.0)
    return (base * row_scale * col_scale).astype(jnp.bfloat16)


def draw_enc_rows(key, part):
    first = jax.random.fold_in(key, 0)
    shape = (PRODUCTS, ELEN, D)
    base = jnp.clip(jax.random.normal(first, shape, jnp.float32), -4.0, 4.0)
    return base.astype(jnp.bfloat16)


def draw_tile_mask(key, part):
    first, second = jax.random.split(key, 2)
    bits = jax.random.randint(first, (PRODUCTS, CANDS, ETILES), 0, 2)
    forced = jax.random.randint(second, (PRODUCTS, CANDS, 1), 0, ETILES)
    places = jnp.arange(ETILES).astype(jnp.int32)[None, None, :]
    return jnp.maximum(bits, (places == forced).astype(jnp.int32)).astype(jnp.int32)


def draw_counts(key, part):
    first, second = jax.random.split(key, 2)
    filled = jax.random.randint(first, (PRODUCTS,), 1, CANDS + 1)
    chosen = jax.random.randint(second, (), 0, PRODUCTS)
    places = jnp.arange(PRODUCTS).astype(jnp.int32)
    return jnp.where(places == chosen, CANDS, filled).astype(jnp.int32)


def block_scale(rng, dims, cuts, least, top_value):
    gain, own = 1.0, jax.random.fold_in(rng, 6)
    for position, shards_of in cuts:
        steps = jnp.exp(jax.random.uniform(jax.random.fold_in(own, position), (shards_of,), jnp.float32, least / len(cuts), top_value / len(cuts)))
        gain = gain * jnp.repeat(steps, dims[position] // shards_of).reshape([-1 if axis == position else 1 for axis in range(len(dims))])
    return gain


def noise(key, dims, width, limit, cuts=(), held_as=jnp.bfloat16):
    drawn = width * jax.random.normal(key, dims, jnp.float32)
    if cuts:
        drawn = drawn * block_scale(key, dims, cuts, -0.22, 0.18)
    return jnp.clip(drawn, -limit, limit).astype(held_as)


def setup_inputs(seed: int = 0) -> dict:
    arg_keys = jax.random.split(jax.random.key(seed), 9)
    cand_states = draw_cand_states(jax.random.fold_in(arg_keys[8], 71), 0)
    enc_rows = draw_enc_rows(jax.random.fold_in(arg_keys[8], 71), 0)
    w_query = noise(arg_keys[2], (D, D), D ** -0.5, 0.09375, ((0, 4), (1, 8)))
    w_key = noise(arg_keys[3], (D, D), D ** -0.5, 0.09375, ((0, 4), (1, 8)))
    w_value = noise(arg_keys[4], (D, D), D ** -0.5, 0.09375, ((0, 4), (1, 8)))
    w_out = noise(arg_keys[5], (D, D), (HD * 4) ** -0.5, 0.375, ((0, 8), (1, 4)))
    tile_mask = draw_tile_mask(jax.random.fold_in(arg_keys[8], 71), 0)
    counts = draw_counts(jax.random.fold_in(arg_keys[8], 71), 0)
    return dict(cand_states=cand_states, enc_rows=enc_rows, w_query=w_query, w_key=w_key, w_value=w_value, w_out=w_out, tile_mask=tile_mask, counts=counts)


def normalize(rows):
    values = rows.astype(jnp.float32)
    scale = lax.rsqrt(lax.optimization_barrier(jnp.mean(values * values, axis=-1, keepdims=True)) + 1e-06)
    return (values * scale).astype(jnp.bfloat16)

def reference(cand_states, enc_rows, w_query, w_key, w_value, w_out, tile_mask, counts):
    key_tile = (jnp.arange(ELEN) // TILE).astype(jnp.int32)

    def one_product(items):
        states, encoder, flags, count = items
        normed = normalize(states).reshape(CANDS * CLEN, D)
        query = jnp.dot(normed, w_query, preferred_element_type=jnp.float32).astype(jnp.bfloat16)
        keys = jnp.dot(encoder, w_key, preferred_element_type=jnp.float32).astype(jnp.bfloat16)
        values = jnp.dot(encoder, w_value, preferred_element_type=jnp.float32).astype(jnp.bfloat16)
        query = query.reshape(CANDS, CLEN, HEADS, HD).astype(jnp.float32)
        keys = keys.reshape(ELEN, HEADS, HD).astype(jnp.float32)
        values = values.reshape(ELEN, HEADS, HD).astype(jnp.float32)
        scores = jnp.einsum('clhd,ehd->chle', query, keys) * 0.125
        open_keys = flags[:, key_tile] > 0
        scores = jnp.where(open_keys[:, None, None, :], scores, -1e+30)
        top = lax.optimization_barrier(jnp.max(scores, axis=-1, keepdims=True))
        weights = jnp.exp(scores - top)
        probs = (weights / lax.optimization_barrier(jnp.sum(weights, axis=-1, keepdims=True))).astype(jnp.bfloat16)
        context = jnp.einsum('chle,ehd->clhd', probs.astype(jnp.float32), values).astype(jnp.bfloat16)
        context = context.reshape(CANDS * CLEN, D)

        def add_group(index, total):
            start = (index * GROUP).astype(jnp.int32)
            left = lax.dynamic_slice_in_dim(context, start, GROUP, 1)
            right = lax.dynamic_slice_in_dim(w_out, start, GROUP, 0)
            term = lax.optimization_barrier(jnp.dot(left, right, preferred_element_type=jnp.float32).astype(jnp.bfloat16))
            return total + term.astype(jnp.float32)
        total = lax.fori_loop(0, N_CAND, add_group, jnp.zeros((CANDS * CLEN, D), jnp.float32))
        live = (jnp.arange(CANDS).astype(jnp.int32) < count).astype(jnp.float32)
        return (total.reshape(CANDS, CLEN, D) * live[:, None, None]).astype(jnp.bfloat16)
    return lax.map(one_product, (cand_states, enc_rows, tile_mask, counts))
```

```python
import functools

import jax
import jax.numpy as jnp
from jax import lax
from jax.experimental import pallas as pl
from jax.experimental.pallas import tpu as pltpu
from jax.sharding import PartitionSpec as P

HD = 64
TILE = 128
LANES = 128
FLAG_ROWS = 16
VMEM = pltpu.CompilerParams(vmem_limit_bytes=40 * 1024 * 1024)


def ring_order(chips):
    odd = list(range(1, chips, 2))
    even = list(range(2, chips, 2))
    return [0] + odd + even[::-1]


def cost(flops, moved, exps=0):
    return pl.CostEstimate(flops=flops, bytes_accessed=moved, transcendentals=exps)


def normalize_kernel(place, x_ref, out_ref):
    values = x_ref[...].astype(jnp.float32)
    width = values.shape[1]
    scale = lax.rsqrt(jnp.sum(values * values, axis=-1, keepdims=True) / width + 1e-06)
    parts = place.shape[0]
    block = width // parts
    for r in range(parts):
        source = pl.ds(pl.multiple_of(place[r] * block, block), block)
        rows = x_ref[:, source].astype(jnp.float32)
        out_ref[:, r * block : (r + 1) * block] = (rows * scale).astype(jnp.bfloat16)


def normalize(x, place):
    return pl.pallas_call(
        normalize_kernel,
        out_shape=jax.ShapeDtypeStruct(x.shape, jnp.bfloat16),
        in_specs=[
            pl.BlockSpec(memory_space=pltpu.SMEM),
            pl.BlockSpec(memory_space=pltpu.VMEM),
        ],
        out_specs=pl.BlockSpec(memory_space=pltpu.VMEM),
        compiler_params=VMEM,
        cost_estimate=cost(4 * x.size, 4 * x.size),
        name="normalize",
    )(place, x)


def key_value_kernel(slots, parts, rows, *refs):
    pieces, w_key, w_value = refs[:slots], refs[slots], refs[slots + 1]
    outs = refs[slots + 2 :]
    local = w_key.shape[1]
    encoder = jnp.concatenate([piece[: parts * rows, :] for piece in pieces], axis=0)
    for column, weight in ((0, w_key), (local, w_value)):
        sums = jnp.dot(encoder, weight[...], preferred_element_type=jnp.float32)
        for slot in range(slots):
            for r in range(parts):
                start = (slot * parts + r) * rows
                outs[r][slot * rows : (slot + 1) * rows, column : column + local] = sums[
                    start : start + rows
                ].astype(outs[r].dtype)


def key_value(pieces, w_key, w_value, parts, rows):
    slots, local = len(pieces), w_key.shape[1]
    shape = (slots * rows, 2 * local)
    flops = 2 * slots * parts * rows * w_key.shape[0] * 2 * local
    return pl.pallas_call(
        functools.partial(key_value_kernel, slots, parts, rows),
        out_shape=[
            jax.ShapeDtypeStruct(shape, jnp.float32 if r == 0 else jnp.bfloat16)
            for r in range(parts)
        ],
        in_specs=[pl.BlockSpec(memory_space=pltpu.VMEM)] * (slots + 2),
        out_specs=[pl.BlockSpec(memory_space=pltpu.VMEM)] * parts,
        compiler_params=VMEM,
        cost_estimate=cost(flops, 8 * 1024 * 1024),
        name="key_value",
    )(*pieces, w_key, w_value)


def attend_kernel(pieces, heads, mine, sib, open_ref, kv_ref, *refs):
    weights, out_ref = refs[:pieces], refs[pieces]
    clen = mine.shape[0]
    depth = weights[0].shape[0]
    local = heads * HD
    total = None
    for index, weight in enumerate(weights):
        columns = slice(index * depth, (index + 1) * depth)
        rows = jnp.concatenate([mine[:, columns], sib[:, columns]], axis=0)
        term = jnp.dot(rows, weight[...], preferred_element_type=jnp.float32)
        total = term if total is None else total + term
    query = total.astype(jnp.bfloat16)
    elen = kv_ref.shape[0]
    is_open = (
        jnp.concatenate(
            [jnp.broadcast_to(open_ref[i : i + 1, :], (clen, elen)) for i in range(2)], axis=0
        )
        > 0.5
    )
    lane = lax.broadcasted_iota(jnp.int32, (elen, LANES), 1) // HD
    for pair in range(local // LANES):
        columns = slice(pair * LANES, (pair + 1) * LANES)
        keys = kv_ref[:, columns]
        values = kv_ref[:, local + pair * LANES : local + (pair + 1) * LANES]
        context = None
        for half in range(LANES // HD):
            own = lane == half
            scores = (
                lax.dot_general(
                    query[:, columns],
                    jnp.where(own, keys, jnp.zeros_like(keys)),
                    (((1,), (1,)), ((), ())),
                    preferred_element_type=jnp.float32,
                )
                * 0.125
            )
            scores = jnp.where(is_open, scores, -1e30)
            top = jnp.max(scores, axis=-1, keepdims=True)
            grown = jnp.exp(scores - top)
            probs = (grown / jnp.sum(grown, axis=-1, keepdims=True)).astype(jnp.bfloat16)
            term = jnp.dot(
                probs,
                jnp.where(own, values, jnp.zeros_like(values)),
                preferred_element_type=jnp.float32,
            )
            context = term if context is None else context + term
        out_ref[:, columns] = context.astype(jnp.bfloat16)


def attend(mine, sib, is_open, kv, weights):
    clen, width = mine.shape
    elen, local = kv.shape[0], kv.shape[1] // 2
    flops = 2 * 2 * clen * (width * local + 2 * elen * local)
    return pl.pallas_call(
        functools.partial(attend_kernel, len(weights), local // HD),
        out_shape=jax.ShapeDtypeStruct((2 * clen, local), jnp.bfloat16),
        in_specs=[pl.BlockSpec(memory_space=pltpu.VMEM)] * (4 + len(weights)),
        out_specs=pl.BlockSpec(memory_space=pltpu.VMEM),
        compiler_params=VMEM,
        cost_estimate=cost(flops, 2 * width * (2 * clen + local), 2 * clen * elen * local // HD),
        name="attend",
    )(mine, sib, is_open, kv, *weights)


def project_kernel(parts, context_ref, *refs):
    weights, (mine, sib) = refs[: 2 * parts], refs[2 * parts :]
    clen = mine.shape[0]
    depth, block = weights[0].shape
    for r in range(parts):
        total = None
        for half in range(2):
            term = jnp.dot(
                context_ref[:, half * depth : (half + 1) * depth],
                weights[2 * r + half][...],
                preferred_element_type=jnp.float32,
            )
            total = term if total is None else total + term
        rows = total.astype(jnp.bfloat16)
        mine[:, r * block : (r + 1) * block] = rows[:clen]
        sib[:, r * block : (r + 1) * block] = rows[clen:]


def project(context, weights):
    parts = len(weights) // 2
    rows, local = context.shape
    width = parts * weights[0].shape[1]
    shape = jax.ShapeDtypeStruct((rows // 2, width), jnp.bfloat16)
    return pl.pallas_call(
        functools.partial(project_kernel, parts),
        out_shape=[shape, shape],
        in_specs=[pl.BlockSpec(memory_space=pltpu.VMEM)] * (1 + len(weights)),
        out_specs=[pl.BlockSpec(memory_space=pltpu.VMEM)] * 2,
        compiler_params=VMEM,
        cost_estimate=cost(2 * rows * local * width, 2 * width * (rows + local)),
        name="project",
    )(context, *weights)


def finish_kernel(place, live, mine, other, passed, out_ref):
    parts = place.shape[0]
    block = out_ref.shape[1] // parts
    for r in range(parts):
        columns = slice(r * block, (r + 1) * block)
        total = mine[:, columns].astype(jnp.float32) + other[:, columns].astype(jnp.float32)
        total = total + passed[:, columns].astype(jnp.float32)
        target = pl.ds(pl.multiple_of(place[r] * block, block), block)
        out_ref[:, target] = (total * live[0]).astype(jnp.bfloat16)


def finish(place, live, mine, other, passed):
    return pl.pallas_call(
        finish_kernel,
        out_shape=jax.ShapeDtypeStruct(mine.shape, jnp.bfloat16),
        in_specs=[pl.BlockSpec(memory_space=pltpu.SMEM)] * 2
        + [pl.BlockSpec(memory_space=pltpu.VMEM)] * 3,
        out_specs=pl.BlockSpec(memory_space=pltpu.VMEM),
        compiler_params=VMEM,
        cost_estimate=cost(4 * mine.size, 8 * mine.size),
        name="finish",
    )(place, live, mine, other, passed)


def shards(parts, devices, cand_states, enc_rows, w_query, w_key, w_value, w_out, tile_mask, counts):
    chips = devices // 2
    order = ring_order(chips)
    along = [
        (2 * order[i] + core, 2 * order[(i + 1) % chips] + core)
        for i in range(chips)
        for core in range(2)
    ]
    across = [(c, c ^ 1) for c in range(devices)]

    def to_next(value):
        return lax.ppermute(value, "cand", along)

    def to_sib(value):
        return lax.ppermute(value, "cand", across)

    def flip(value, r):
        return lax.ppermute(value, "prod", [(q, q ^ r) for q in range(parts)])

    def spread(weight):
        bits = [1 << b for b in range(parts.bit_length() - 1)]
        depth = weight.shape[0] // 2
        halves = []
        for half, way in ((0, bits), (1, bits[::-1])):
            held = {0: weight[half * depth : (half + 1) * depth]}
            for bit in way:
                held.update({r ^ bit: flip(piece, bit) for r, piece in held.items()})
            halves.append(held)
        return [halves[half][r] for r in range(parts) for half in range(2)]

    me_prod = lax.axis_index("prod")
    me = lax.axis_index("cand")
    place = jnp.bitwise_xor(me_prod, jnp.arange(parts, dtype=jnp.int32))

    rows, width = enc_rows.shape[1:]
    block = width // parts
    encoder = enc_rows.reshape(rows, width)
    columns = [
        lax.dynamic_slice_in_dim(encoder, place[r] * block, block, 1) for r in range(parts)
    ]
    columns = [columns[0]] + [flip(columns[r], r) for r in range(1, parts)]
    tiles = tile_mask.shape[2]
    flags = tile_mask.reshape(1, tiles, 1).astype(jnp.bfloat16)
    flags = jnp.broadcast_to(flags, (FLAG_ROWS, tiles, block // tiles)).reshape(FLAG_ROWS, block)
    piece = jnp.concatenate(columns + [flags], axis=0)
    pieces = [piece, to_sib(piece)]
    for _ in range(1, chips):
        piece = to_next(piece)
        pieces += [piece, to_sib(piece)]

    clen = cand_states.shape[2]
    normed = normalize(cand_states.reshape(clen, width), place)
    pairs = [(normed, to_sib(normed))]
    for _ in range(1, chips):
        normed = to_next(normed)
        pairs.append((normed, to_sib(normed)))

    query_parts = spread(w_query)
    out_parts = spread(w_out)

    sums = key_value(pieces, w_key, w_value, parts, rows)
    kv = sums[0]
    for r in range(1, parts):
        kv = kv + flip(sums[r], r).astype(jnp.float32)
    kv = kv.astype(jnp.bfloat16)

    where_in_ring = jnp.array([order.index(chip) for chip in range(chips)], jnp.int32)
    chip_at = jnp.array(order, jnp.int32)
    steps = jnp.arange(chips, dtype=jnp.int32)
    chip_of = chip_at[(where_in_ring[me // 2] - steps + chips) % chips]
    core = jnp.stack([me % 2, 1 - me % 2])
    source = (2 * chip_of[:, None] + core[None, :]).reshape(devices)
    key_tile = ((source * rows)[:, None] + jnp.arange(rows)[None, :]).reshape(-1) // TILE
    seen = jnp.stack([p[parts * rows, :: block // tiles] for p in pieces]).astype(jnp.float32)
    match = (key_tile[None, :] == jnp.arange(tiles)[:, None]).astype(jnp.float32)
    is_open = jnp.sum(seen[:, :, None] * match[None, :, :], axis=1)

    passed = None
    for step in list(range(1, chips)) + [0]:
        mine, sib = pairs[step]
        context = attend(mine, sib, is_open[2 * step : 2 * step + 2], kv, query_parts)
        mine_sum, sib_sum = project(context, out_parts)
        other = to_sib(sib_sum)
        if step:
            total = mine_sum.astype(jnp.float32) + other.astype(jnp.float32)
            if passed is not None:
                total = total + passed.astype(jnp.float32)
            passed = to_next(total.astype(jnp.bfloat16))
    live = (me < counts).astype(jnp.float32)
    return finish(place, live, mine_sum, other, passed).reshape(cand_states.shape)


def solution(mesh):
    parts, devices = mesh.shape["prod"], mesh.shape["cand"]
    return jax.shard_map(
        functools.partial(shards, parts, devices),
        mesh=mesh,
        in_specs=(
            P("prod", "cand", None, None),
            P("prod", "cand", None),
            P("prod", "cand"),
            P("prod", "cand"),
            P("prod", "cand"),
            P("cand", "prod"),
            P("prod", "cand", None),
            P("prod"),
        ),
        out_specs=P("prod", "cand", None, None),
        check_vma=False,
    )
```

```python
import functools

import jax
import jax.numpy as jnp
from jax import lax
from jax.experimental import pallas as pl
from jax.experimental.pallas import tpu as pltpu
from jax.sharding import PartitionSpec as P

HD = 64
TILE = 128
LANES = 128
FLAG_ROWS = 16
VMEM = pltpu.CompilerParams(vmem_limit_bytes=40 * 1024 * 1024)


def ring_order(chips):
    odd = list(range(1, chips, 2))
    even = list(range(2, chips, 2))
    return [0] + odd + even[::-1]


def small():
    return pl.CostEstimate(flops=1, bytes_accessed=1, transcendentals=0)


def key_value_kernel(parts, rows, tiles, tile_of, enc_ref, w_key, w_value, open_ref, *outs):
    slots, height, block = enc_ref.shape
    local = w_key.shape[1]
    encoder = jnp.concatenate([enc_ref[slot, : parts * rows, :] for slot in range(slots)], axis=0)
    for column, weight in ((0, w_key), (local, w_value)):
        sums = jnp.dot(encoder, weight[...], preferred_element_type=jnp.float32)
        for slot in range(slots):
            for r in range(parts):
                start = (slot * parts + r) * rows
                outs[r][slot * rows : (slot + 1) * rows, column : column + local] = sums[
                    start : start + rows
                ].astype(outs[r].dtype)
    elen = slots * rows
    tile = lax.broadcasted_iota(jnp.int32, (1, elen), 1) // tile_of
    for slot in range(slots):
        seen = jnp.zeros((1, elen), jnp.float32)
        for t in range(tiles):
            start = t * (block // tiles)
            flag = enc_ref[slot, height - 1 : height, start : start + elen].astype(jnp.float32)
            seen = jnp.where(tile == t, flag, seen)
        open_ref[slot : slot + 1, :] = seen


def key_value(gathered, w_key, w_value, parts, rows, tiles):
    slots, local = gathered.shape[0], w_key.shape[1]
    elen = slots * rows
    return pl.pallas_call(
        functools.partial(key_value_kernel, parts, rows, tiles, TILE),
        out_shape=[jax.ShapeDtypeStruct((slots, elen), jnp.float32)]
        + [
            jax.ShapeDtypeStruct((elen, 2 * local), jnp.float32 if r == 0 else jnp.bfloat16)
            for r in range(parts)
        ],
        in_specs=[pl.BlockSpec(memory_space=pltpu.VMEM)] * 3,
        out_specs=[pl.BlockSpec(memory_space=pltpu.VMEM)] * (parts + 1),
        compiler_params=VMEM,
        cost_estimate=small(),
        name="key_value",
    )(gathered, w_key, w_value)


def query_kernel(pieces, place, mine, sib, *refs):
    weights, out_ref = refs[:pieces], refs[pieces]
    parts = place.shape[0]
    clen, width = mine.shape
    block = width // parts
    scales = []
    for ref in (mine, sib):
        values = ref[...].astype(jnp.float32)
        scales.append(lax.rsqrt(jnp.sum(values * values, axis=-1, keepdims=True) / width + 1e-06))
    total, start = None, 0
    for weight in weights:
        depth = weight.shape[0]
        source = pl.multiple_of(place[start // block] * block + start % block, LANES)
        rows = jnp.concatenate(
            [
                (ref[:, pl.ds(source, depth)].astype(jnp.float32) * scale).astype(jnp.bfloat16)
                for ref, scale in zip((mine, sib), scales)
            ],
            axis=0,
        )
        term = jnp.dot(rows, weight[...], preferred_element_type=jnp.float32)
        total = term if total is None else total + term
        start += depth
    out_ref[...] = total.astype(jnp.bfloat16)


def query(place, mine, sib, weights):
    clen = mine.shape[0]
    return pl.pallas_call(
        functools.partial(query_kernel, len(weights)),
        out_shape=jax.ShapeDtypeStruct((2 * clen, weights[0].shape[1]), jnp.bfloat16),
        in_specs=[pl.BlockSpec(memory_space=pltpu.SMEM)]
        + [pl.BlockSpec(memory_space=pltpu.VMEM)] * (2 + len(weights)),
        out_specs=pl.BlockSpec(memory_space=pltpu.VMEM),
        compiler_params=VMEM,
        cost_estimate=small(),
        name="query",
    )(place, mine, sib, *weights)


def attend_kernel(who, query_ref, open_ref, kv_ref, out_ref):
    clen = query_ref.shape[0] // 2
    elen, local = kv_ref.shape[0], kv_ref.shape[1] // 2
    is_open = (
        jnp.concatenate(
            [jnp.broadcast_to(open_ref[pl.ds(who[i], 1), :], (clen, elen)) for i in range(2)],
            axis=0,
        )
        > 0.5
    )
    lane = lax.broadcasted_iota(jnp.int32, (elen, LANES), 1) // HD
    for pair in range(local // LANES):
        columns = slice(pair * LANES, (pair + 1) * LANES)
        keys = kv_ref[:, columns]
        values = kv_ref[:, local + pair * LANES : local + (pair + 1) * LANES]
        context = None
        for half in range(LANES // HD):
            own = lane == half
            scores = (
                lax.dot_general(
                    query_ref[:, columns],
                    jnp.where(own, keys, jnp.zeros_like(keys)),
                    (((1,), (1,)), ((), ())),
                    preferred_element_type=jnp.float32,
                )
                * 0.125
            )
            scores = jnp.where(is_open, scores, -1e30)
            top = jnp.max(scores, axis=-1, keepdims=True)
            grown = jnp.exp(scores - top)
            probs = (grown / jnp.sum(grown, axis=-1, keepdims=True)).astype(jnp.bfloat16)
            term = jnp.dot(
                probs,
                jnp.where(own, values, jnp.zeros_like(values)),
                preferred_element_type=jnp.float32,
            )
            context = term if context is None else context + term
        out_ref[:, columns] = context.astype(jnp.bfloat16)


def attend(who, queries, is_open, kv):
    return pl.pallas_call(
        attend_kernel,
        out_shape=jax.ShapeDtypeStruct(queries.shape, jnp.bfloat16),
        in_specs=[pl.BlockSpec(memory_space=pltpu.SMEM)]
        + [pl.BlockSpec(memory_space=pltpu.VMEM)] * 3,
        out_specs=pl.BlockSpec(memory_space=pltpu.VMEM),
        compiler_params=VMEM,
        cost_estimate=small(),
        name="attend",
    )(who, queries, is_open, kv)


def project_kernel(pieces, context_ref, *refs):
    weights, (mine, sib) = refs[: len(pieces)], refs[len(pieces) :]
    clen = mine.shape[0]
    totals = {}
    for (r, row), weight in zip(pieces, weights):
        term = jnp.dot(
            context_ref[:, row : row + weight.shape[0]],
            weight[...],
            preferred_element_type=jnp.float32,
        )
        totals[r] = term if r not in totals else totals[r] + term
        if row + weight.shape[0] == context_ref.shape[1]:
            block = weight.shape[1]
            rows = totals[r].astype(jnp.bfloat16)
            mine[:, r * block : (r + 1) * block] = rows[:clen]
            sib[:, r * block : (r + 1) * block] = rows[clen:]


def project(context, weights, parts):
    rows, local = context.shape
    pieces, row = [], 0
    for weight in weights:
        pieces.append((row // local, row % local))
        row += weight.shape[0]
    width = parts * weights[0].shape[1]
    shape = jax.ShapeDtypeStruct((rows // 2, width), jnp.bfloat16)
    return pl.pallas_call(
        functools.partial(project_kernel, pieces),
        out_shape=[shape, shape],
        in_specs=[pl.BlockSpec(memory_space=pltpu.VMEM)] * (1 + len(weights)),
        out_specs=[pl.BlockSpec(memory_space=pltpu.VMEM)] * 2,
        compiler_params=VMEM,
        cost_estimate=small(),
        name="project",
    )(context, *weights)


def finish_kernel(place, live, mine, other, passed, out_ref):
    parts = place.shape[0]
    block = out_ref.shape[1] // parts
    for r in range(parts):
        columns = slice(r * block, (r + 1) * block)
        total = mine[:, columns].astype(jnp.float32) + other[:, columns].astype(jnp.float32)
        total = total + passed[:, columns].astype(jnp.float32)
        target = pl.ds(pl.multiple_of(place[r] * block, block), block)
        out_ref[:, target] = (total * live[0]).astype(jnp.bfloat16)


def finish(place, live, mine, other, passed):
    return pl.pallas_call(
        finish_kernel,
        out_shape=jax.ShapeDtypeStruct(mine.shape, jnp.bfloat16),
        in_specs=[pl.BlockSpec(memory_space=pltpu.SMEM)] * 2
        + [pl.BlockSpec(memory_space=pltpu.VMEM)] * 3,
        out_specs=pl.BlockSpec(memory_space=pltpu.VMEM),
        compiler_params=VMEM,
        cost_estimate=small(),
        name="finish",
    )(place, live, mine, other, passed)


def shards(parts, devices, cand_states, enc_rows, w_query, w_key, w_value, w_out, tile_mask, counts):
    chips = devices // 2
    order = ring_order(chips)
    along = [
        (2 * order[i] + core, 2 * order[(i + 1) % chips] + core)
        for i in range(chips)
        for core in range(2)
    ]
    across = [(c, c ^ 1) for c in range(devices)]

    def to_next(value):
        return lax.ppermute(value, "cand", along)

    def to_sib(value):
        return lax.ppermute(value, "cand", across)

    def flip(value, r):
        return lax.ppermute(value, "prod", [(q, q ^ r) for q in range(parts)])

    def spread(weight):
        if parts != 4:
            return [weight] + [flip(weight, r) for r in range(1, parts)]
        first, second = flip(weight, 1), flip(weight, 2)
        half = weight.shape[0] // 2
        corner = [flip(first[:half], 2), flip(second[half:], 1)]
        return [weight, first, second] + corner

    me_prod = lax.axis_index("prod")
    me = lax.axis_index("cand")
    place = jnp.bitwise_xor(me_prod, jnp.arange(parts, dtype=jnp.int32))

    clen, width = cand_states.shape[2:]
    states = cand_states.reshape(clen, width)
    pairs = [(states, to_sib(states))]
    for _ in range(1, chips):
        states = to_next(states)
        pairs.append((states, to_sib(states)))

    rows = enc_rows.shape[1]
    block = width // parts
    encoder = enc_rows.reshape(rows, width)
    columns = [
        lax.dynamic_slice_in_dim(encoder, place[r] * block, block, 1) for r in range(parts)
    ]
    columns = [columns[0]] + [flip(columns[r], r) for r in range(1, parts)]
    tiles = tile_mask.shape[2]
    flags = tile_mask.reshape(1, tiles, 1).astype(jnp.bfloat16)
    flags = jnp.broadcast_to(flags, (FLAG_ROWS, tiles, block // tiles)).reshape(FLAG_ROWS, block)
    piece = jnp.concatenate(columns + [flags], axis=0)
    gathered = lax.all_gather(piece, "cand", axis=0)

    query_parts = spread(w_query)
    query_parts, w_out = lax.optimization_barrier((query_parts, w_out))
    out_parts = spread(w_out)

    is_open, *sums = key_value(gathered, w_key, w_value, parts, rows, tiles)
    kv = sums[0]
    for r in range(1, parts):
        kv = kv + flip(sums[r], r).astype(jnp.float32)
    kv = kv.astype(jnp.bfloat16)

    where_in_ring = jnp.array([order.index(chip) for chip in range(chips)], jnp.int32)
    chip_at = jnp.array(order, jnp.int32)
    steps = jnp.arange(chips, dtype=jnp.int32)
    chip_of = chip_at[(where_in_ring[me // 2] - steps + chips) % chips]
    core = jnp.stack([me % 2, 1 - me % 2])
    who = 2 * chip_of[:, None] + core[None, :]

    passed = None
    for step in list(range(1, chips)) + [0]:
        queries = query(place, *pairs[step], query_parts)
        context = attend(who[step], queries, is_open, kv)
        mine_sum, sib_sum = project(context, out_parts, parts)
        other = to_sib(sib_sum)
        if step:
            total = mine_sum.astype(jnp.float32) + other.astype(jnp.float32)
            if passed is not None:
                total = total + passed.astype(jnp.float32)
            passed = to_next(total.astype(jnp.bfloat16))
    live = (me < counts).astype(jnp.float32)
    return finish(place, live, mine_sum, other, passed).reshape(cand_states.shape)


def solution(mesh):
    parts, devices = mesh.shape["prod"], mesh.shape["cand"]
    return jax.shard_map(
        functools.partial(shards, parts, devices),
        mesh=mesh,
        in_specs=(
            P("prod", "cand", None, None),
            P("prod", "cand", None),
            P("prod", "cand"),
            P("prod", "cand"),
            P("prod", "cand"),
            P("cand", "prod"),
            P("prod", "cand", None),
            P("prod"),
        ),
        out_specs=P("prod", "cand", None, None),
        check_vma=False,
    )
```

```python
import functools

import jax
import jax.numpy as jnp
from jax import lax
from jax.experimental import pallas as pl
from jax.experimental.pallas import tpu as pltpu
from jax.sharding import PartitionSpec as P

HD = 64
TILE = 128
LANES = 128
FLAG_ROWS = 16
VMEM = pltpu.CompilerParams(vmem_limit_bytes=40 * 1024 * 1024)


def ring_order(chips):
    odd = list(range(1, chips, 2))
    even = list(range(2, chips, 2))
    return [0] + odd + even[::-1]


def small():
    return pl.CostEstimate(flops=1, bytes_accessed=1, transcendentals=0)


def key_value_kernel(parts, rows, tiles, tile_of, enc_ref, w_key, w_value, open_ref, *outs):
    slots, height, block = enc_ref.shape
    local = w_key.shape[1]
    encoder = jnp.concatenate([enc_ref[slot, : parts * rows, :] for slot in range(slots)], axis=0)
    for column, weight in ((0, w_key), (local, w_value)):
        sums = jnp.dot(encoder, weight[...], preferred_element_type=jnp.float32)
        for slot in range(slots):
            for r in range(parts):
                start = (slot * parts + r) * rows
                outs[r][slot * rows : (slot + 1) * rows, column : column + local] = sums[
                    start : start + rows
                ].astype(outs[r].dtype)
    elen = slots * rows
    tile = lax.broadcasted_iota(jnp.int32, (1, elen), 1) // tile_of
    for slot in range(slots):
        seen = jnp.zeros((1, elen), jnp.float32)
        for t in range(tiles):
            start = t * (block // tiles)
            flag = enc_ref[slot, height - 1 : height, start : start + elen].astype(jnp.float32)
            seen = jnp.where(tile == t, flag, seen)
        open_ref[slot : slot + 1, :] = seen


def key_value(gathered, w_key, w_value, parts, rows, tiles):
    slots, local = gathered.shape[0], w_key.shape[1]
    elen = slots * rows
    return pl.pallas_call(
        functools.partial(key_value_kernel, parts, rows, tiles, TILE),
        out_shape=[jax.ShapeDtypeStruct((slots, elen), jnp.float32)]
        + [
            jax.ShapeDtypeStruct((elen, 2 * local), jnp.float32 if r == 0 else jnp.bfloat16)
            for r in range(parts)
        ],
        in_specs=[pl.BlockSpec(memory_space=pltpu.VMEM)] * 3,
        out_specs=[pl.BlockSpec(memory_space=pltpu.VMEM)] * (parts + 1),
        compiler_params=VMEM,
        cost_estimate=small(),
        name="key_value",
    )(gathered, w_key, w_value)


def query_kernel(pieces, place, mine, sib, *refs):
    weights, out_ref = refs[:pieces], refs[pieces]
    parts = place.shape[0]
    clen, width = mine.shape
    block = width // parts
    scales = []
    for ref in (mine, sib):
        values = ref[...].astype(jnp.float32)
        scales.append(lax.rsqrt(jnp.sum(values * values, axis=-1, keepdims=True) / width + 1e-06))
    total, start = None, 0
    for weight in weights:
        depth = weight.shape[0]
        source = pl.multiple_of(place[start // block] * block + start % block, LANES)
        rows = jnp.concatenate(
            [
                (ref[:, pl.ds(source, depth)].astype(jnp.float32) * scale).astype(jnp.bfloat16)
                for ref, scale in zip((mine, sib), scales)
            ],
            axis=0,
        )
        term = jnp.dot(rows, weight[...], preferred_element_type=jnp.float32)
        total = term if total is None else total + term
        start += depth
    out_ref[...] = total.astype(jnp.bfloat16)


def query(place, mine, sib, weights):
    clen = mine.shape[0]
    return pl.pallas_call(
        functools.partial(query_kernel, len(weights)),
        out_shape=jax.ShapeDtypeStruct((2 * clen, weights[0].shape[1]), jnp.bfloat16),
        in_specs=[pl.BlockSpec(memory_space=pltpu.SMEM)]
        + [pl.BlockSpec(memory_space=pltpu.VMEM)] * (2 + len(weights)),
        out_specs=pl.BlockSpec(memory_space=pltpu.VMEM),
        compiler_params=VMEM,
        cost_estimate=small(),
        name="query",
    )(place, mine, sib, *weights)


def attend_kernel(who, query_ref, open_ref, kv_ref, out_ref):
    clen = query_ref.shape[0] // 2
    elen, local = kv_ref.shape[0], kv_ref.shape[1] // 2
    is_open = (
        jnp.concatenate(
            [jnp.broadcast_to(open_ref[pl.ds(who[i], 1), :], (clen, elen)) for i in range(2)],
            axis=0,
        )
        > 0.5
    )
    lane = lax.broadcasted_iota(jnp.int32, (elen, LANES), 1) // HD
    for pair in range(local // LANES):
        columns = slice(pair * LANES, (pair + 1) * LANES)
        keys = kv_ref[:, columns]
        values = kv_ref[:, local + pair * LANES : local + (pair + 1) * LANES]
        context = None
        for half in range(LANES // HD):
            own = lane == half
            scores = (
                lax.dot_general(
                    query_ref[:, columns],
                    jnp.where(own, keys, jnp.zeros_like(keys)),
                    (((1,), (1,)), ((), ())),
                    preferred_element_type=jnp.float32,
                )
                * 0.125
            )
            scores = jnp.where(is_open, scores, -1e30)
            top = jnp.max(scores, axis=-1, keepdims=True)
            grown = jnp.exp(scores - top)
            probs = (grown / jnp.sum(grown, axis=-1, keepdims=True)).astype(jnp.bfloat16)
            term = jnp.dot(
                probs,
                jnp.where(own, values, jnp.zeros_like(values)),
                preferred_element_type=jnp.float32,
            )
            context = term if context is None else context + term
        out_ref[:, columns] = context.astype(jnp.bfloat16)


def attend(who, queries, is_open, kv):
    return pl.pallas_call(
        attend_kernel,
        out_shape=jax.ShapeDtypeStruct(queries.shape, jnp.bfloat16),
        in_specs=[pl.BlockSpec(memory_space=pltpu.SMEM)]
        + [pl.BlockSpec(memory_space=pltpu.VMEM)] * 3,
        out_specs=pl.BlockSpec(memory_space=pltpu.VMEM),
        compiler_params=VMEM,
        cost_estimate=small(),
        name="attend",
    )(who, queries, is_open, kv)


def project_kernel(pieces, context_ref, *refs):
    weights, (mine, sib) = refs[: len(pieces)], refs[len(pieces) :]
    clen = mine.shape[0]
    totals = {}
    for (r, row), weight in zip(pieces, weights):
        term = jnp.dot(
            context_ref[:, row : row + weight.shape[0]],
            weight[...],
            preferred_element_type=jnp.float32,
        )
        totals[r] = term if r not in totals else totals[r] + term
        if row + weight.shape[0] == context_ref.shape[1]:
            block = weight.shape[1]
            rows = totals[r].astype(jnp.bfloat16)
            mine[:, r * block : (r + 1) * block] = rows[:clen]
            sib[:, r * block : (r + 1) * block] = rows[clen:]


def project(context, weights, parts):
    rows, local = context.shape
    pieces, row = [], 0
    for weight in weights:
        pieces.append((row // local, row % local))
        row += weight.shape[0]
    width = parts * weights[0].shape[1]
    shape = jax.ShapeDtypeStruct((rows // 2, width), jnp.bfloat16)
    return pl.pallas_call(
        functools.partial(project_kernel, pieces),
        out_shape=[shape, shape],
        in_specs=[pl.BlockSpec(memory_space=pltpu.VMEM)] * (1 + len(weights)),
        out_specs=[pl.BlockSpec(memory_space=pltpu.VMEM)] * 2,
        compiler_params=VMEM,
        cost_estimate=small(),
        name="project",
    )(context, *weights)


def finish_kernel(place, live, mine, other, passed, out_ref):
    parts = place.shape[0]
    block = out_ref.shape[1] // parts
    for r in range(parts):
        columns = slice(r * block, (r + 1) * block)
        total = mine[:, columns].astype(jnp.float32) + other[:, columns].astype(jnp.float32)
        total = total + passed[:, columns].astype(jnp.float32)
        target = pl.ds(pl.multiple_of(place[r] * block, block), block)
        out_ref[:, target] = (total * live[0]).astype(jnp.bfloat16)


def finish(place, live, mine, other, passed):
    return pl.pallas_call(
        finish_kernel,
        out_shape=jax.ShapeDtypeStruct(mine.shape, jnp.bfloat16),
        in_specs=[pl.BlockSpec(memory_space=pltpu.SMEM)] * 2
        + [pl.BlockSpec(memory_space=pltpu.VMEM)] * 3,
        out_specs=pl.BlockSpec(memory_space=pltpu.VMEM),
        compiler_params=VMEM,
        cost_estimate=small(),
        name="finish",
    )(place, live, mine, other, passed)


def shards(parts, devices, cand_states, enc_rows, w_query, w_key, w_value, w_out, tile_mask, counts):
    chips = devices // 2
    order = ring_order(chips)
    along = [
        (2 * order[i] + core, 2 * order[(i + 1) % chips] + core)
        for i in range(chips)
        for core in range(2)
    ]
    across = [(c, c ^ 1) for c in range(devices)]

    def to_next(value):
        return lax.ppermute(value, "cand", along)

    def to_sib(value):
        return lax.ppermute(value, "cand", across)

    def flip(value, r):
        return lax.ppermute(value, "prod", [(q, q ^ r) for q in range(parts)])

    def spread(weight):
        if parts != 4:
            return [weight] + [flip(weight, r) for r in range(1, parts)]
        first, second = flip(weight, 1), flip(weight, 2)
        half = weight.shape[0] // 2
        corner = [flip(first[:half], 2), flip(second[half:], 1)]
        return [weight, first, second] + corner

    me_prod = lax.axis_index("prod")
    me = lax.axis_index("cand")
    place = jnp.bitwise_xor(me_prod, jnp.arange(parts, dtype=jnp.int32))

    clen, width = cand_states.shape[2:]
    states = cand_states.reshape(clen, width)
    pairs = [(states, to_sib(states))]
    top, bottom = to_next(states[: clen // 2]), states[clen // 2 :]

    rows = enc_rows.shape[1]
    block = width // parts
    encoder, pairs[0] = lax.optimization_barrier((enc_rows.reshape(rows, width), pairs[0]))
    columns = [
        lax.dynamic_slice_in_dim(encoder, place[r] * block, block, 1) for r in range(parts)
    ]
    columns = [columns[0]] + [flip(columns[r], r) for r in range(1, parts)]
    tiles = tile_mask.shape[2]
    flags = tile_mask.reshape(1, tiles, 1).astype(jnp.bfloat16)
    flags = jnp.broadcast_to(flags, (FLAG_ROWS, tiles, block // tiles)).reshape(FLAG_ROWS, block)
    piece = jnp.concatenate(columns + [flags], axis=0)
    piece, top = lax.optimization_barrier((piece, top))
    gathered = lax.all_gather(piece, "cand", axis=0)
    states = jnp.concatenate([top, to_next(bottom)], axis=0)
    pairs.append((states, to_sib(states)))
    for _ in range(2, chips):
        states = to_next(states)
        pairs.append((states, to_sib(states)))

    query_parts = spread(w_query)
    query_parts, w_out = lax.optimization_barrier((query_parts, w_out))
    out_parts = spread(w_out)

    is_open, *sums = key_value(gathered, w_key, w_value, parts, rows, tiles)
    kv = sums[0]
    for r in range(1, parts):
        kv = kv + flip(sums[r], r).astype(jnp.float32)
    kv = kv.astype(jnp.bfloat16)

    where_in_ring = jnp.array([order.index(chip) for chip in range(chips)], jnp.int32)
    chip_at = jnp.array(order, jnp.int32)
    steps = jnp.arange(chips, dtype=jnp.int32)
    chip_of = chip_at[(where_in_ring[me // 2] - steps + chips) % chips]
    core = jnp.stack([me % 2, 1 - me % 2])
    who = 2 * chip_of[:, None] + core[None, :]

    passed = None
    for step in list(range(1, chips)) + [0]:
        queries = query(place, *pairs[step], query_parts)
        context = attend(who[step], queries, is_open, kv)
        mine_sum, sib_sum = project(context, out_parts, parts)
        other = to_sib(sib_sum)
        if step:
            total = mine_sum.astype(jnp.float32) + other.astype(jnp.float32)
            if passed is not None:
                total = total + passed.astype(jnp.float32)
            passed = to_next(total.astype(jnp.bfloat16))
    live = (me < counts).astype(jnp.float32)
    return finish(place, live, mine_sum, other, passed).reshape(cand_states.shape)


def solution(mesh):
    parts, devices = mesh.shape["prod"], mesh.shape["cand"]
    return jax.shard_map(
        functools.partial(shards, parts, devices),
        mesh=mesh,
        in_specs=(
            P("prod", "cand", None, None),
            P("prod", "cand", None),
            P("prod", "cand"),
            P("prod", "cand"),
            P("prod", "cand"),
            P("cand", "prod"),
            P("prod", "cand", None),
            P("prod"),
        ),
        out_specs=P("prod", "cand", None, None),
        check_vma=False,
    )
```

```python
import functools

import jax
import jax.numpy as jnp
from jax import lax
from jax.experimental import pallas as pl
from jax.experimental.pallas import tpu as pltpu
from jax.sharding import PartitionSpec as P

HD = 64
TILE = 128
LANES = 128
FLAG_ROWS = 16
VMEM = pltpu.CompilerParams(vmem_limit_bytes=40 * 1024 * 1024)


def ring_order(chips):
    odd = list(range(1, chips, 2))
    even = list(range(2, chips, 2))
    return [0] + odd + even[::-1]


def small():
    return pl.CostEstimate(flops=1, bytes_accessed=1, transcendentals=0)


def columns_kernel(ids, x_ref, *outs):
    block = outs[0].shape[1]
    for r, out in enumerate(outs):
        source = jnp.bitwise_xor(ids[0], r)
        out[...] = x_ref[:, pl.ds(pl.multiple_of(source * block, block), block)]


def column_blocks(ids, x, parts):
    shape = jax.ShapeDtypeStruct((x.shape[0], x.shape[1] // parts), x.dtype)
    return pl.pallas_call(
        columns_kernel,
        out_shape=[shape] * parts,
        in_specs=[
            pl.BlockSpec(memory_space=pltpu.SMEM),
            pl.BlockSpec(memory_space=pltpu.VMEM),
        ],
        out_specs=[pl.BlockSpec(memory_space=pltpu.VMEM)] * parts,
        compiler_params=VMEM,
        cost_estimate=small(),
        name="columns",
    )(ids, x)


def key_value_kernel(parts, rows, tiles, tile_of, enc_ref, w_key, w_value, open_ref, *outs):
    slots, height, block = enc_ref.shape
    local = w_key.shape[1]
    encoder = jnp.concatenate([enc_ref[slot, : parts * rows, :] for slot in range(slots)], axis=0)
    for column, weight in ((0, w_key), (local, w_value)):
        sums = jnp.dot(encoder, weight[...], preferred_element_type=jnp.float32)
        for slot in range(slots):
            for r in range(parts):
                start = (slot * parts + r) * rows
                outs[r][slot * rows : (slot + 1) * rows, column : column + local] = sums[
                    start : start + rows
                ].astype(outs[r].dtype)
    elen = slots * rows
    tile = lax.broadcasted_iota(jnp.int32, (1, elen), 1) // tile_of
    for slot in range(slots):
        seen = jnp.zeros((1, elen), jnp.float32)
        for t in range(tiles):
            start = t * (block // tiles)
            flag = enc_ref[slot, height - 1 : height, start : start + elen].astype(jnp.float32)
            seen = jnp.where(tile == t, flag, seen)
        open_ref[slot : slot + 1, :] = seen


def key_value(gathered, w_key, w_value, parts, rows, tiles):
    slots, local = gathered.shape[0], w_key.shape[1]
    elen = slots * rows
    return pl.pallas_call(
        functools.partial(key_value_kernel, parts, rows, tiles, TILE),
        out_shape=[jax.ShapeDtypeStruct((slots, elen), jnp.float32)]
        + [
            jax.ShapeDtypeStruct((elen, 2 * local), jnp.float32 if r == 0 else jnp.bfloat16)
            for r in range(parts)
        ],
        in_specs=[pl.BlockSpec(memory_space=pltpu.VMEM)] * 3,
        out_specs=[pl.BlockSpec(memory_space=pltpu.VMEM)] * (parts + 1),
        compiler_params=VMEM,
        cost_estimate=small(),
        name="key_value",
    )(gathered, w_key, w_value)


def query_kernel(pieces, parts, ids, mine, sib, *refs):
    weights, out_ref = refs[:pieces], refs[pieces]
    clen, width = mine.shape
    block = width // parts
    scales = []
    for ref in (mine, sib):
        values = ref[...].astype(jnp.float32)
        scales.append(lax.rsqrt(jnp.sum(values * values, axis=-1, keepdims=True) / width + 1e-06))
    total, start = None, 0
    for weight in weights:
        depth = weight.shape[0]
        from_prod = jnp.bitwise_xor(ids[0], start // block)
        source = pl.multiple_of(from_prod * block + start % block, LANES)
        rows = jnp.concatenate(
            [
                (ref[:, pl.ds(source, depth)].astype(jnp.float32) * scale).astype(jnp.bfloat16)
                for ref, scale in zip((mine, sib), scales)
            ],
            axis=0,
        )
        term = jnp.dot(rows, weight[...], preferred_element_type=jnp.float32)
        total = term if total is None else total + term
        start += depth
    out_ref[...] = total.astype(jnp.bfloat16)


def query(ids, mine, sib, weights, parts):
    clen = mine.shape[0]
    return pl.pallas_call(
        functools.partial(query_kernel, len(weights), parts),
        out_shape=jax.ShapeDtypeStruct((2 * clen, weights[0].shape[1]), jnp.bfloat16),
        in_specs=[pl.BlockSpec(memory_space=pltpu.SMEM)]
        + [pl.BlockSpec(memory_space=pltpu.VMEM)] * (2 + len(weights)),
        out_specs=pl.BlockSpec(memory_space=pltpu.VMEM),
        compiler_params=VMEM,
        cost_estimate=small(),
        name="query",
    )(ids, mine, sib, *weights)


def attend_kernel(order, step, ids, query_ref, open_ref, kv_ref, out_ref):
    chips = len(order)
    chip, core = lax.div(ids[1], 2), lax.rem(ids[1], 2)
    source = chip
    if step:
        for place in range(chips):
            source = jnp.where(chip == order[place], order[(place - step) % chips], source)
    who = (2 * source + core, 2 * source + 1 - core)
    clen = query_ref.shape[0] // 2
    elen, local = kv_ref.shape[0], kv_ref.shape[1] // 2
    is_open = (
        jnp.concatenate(
            [jnp.broadcast_to(open_ref[pl.ds(who[i], 1), :], (clen, elen)) for i in range(2)],
            axis=0,
        )
        > 0.5
    )
    lane = lax.broadcasted_iota(jnp.int32, (elen, LANES), 1) // HD
    for pair in range(local // LANES):
        columns = slice(pair * LANES, (pair + 1) * LANES)
        keys = kv_ref[:, columns]
        values = kv_ref[:, local + pair * LANES : local + (pair + 1) * LANES]
        context = None
        for half in range(LANES // HD):
            own = lane == half
            scores = (
                lax.dot_general(
                    query_ref[:, columns],
                    jnp.where(own, keys, jnp.zeros_like(keys)),
                    (((1,), (1,)), ((), ())),
                    preferred_element_type=jnp.float32,
                )
                * 0.125
            )
            scores = jnp.where(is_open, scores, -1e30)
            top = jnp.max(scores, axis=-1, keepdims=True)
            grown = jnp.exp(scores - top)
            probs = (grown / jnp.sum(grown, axis=-1, keepdims=True)).astype(jnp.bfloat16)
            term = jnp.dot(
                probs,
                jnp.where(own, values, jnp.zeros_like(values)),
                preferred_element_type=jnp.float32,
            )
            context = term if context is None else context + term
        out_ref[:, columns] = context.astype(jnp.bfloat16)


def attend(order, step, ids, queries, is_open, kv):
    return pl.pallas_call(
        functools.partial(attend_kernel, order, step),
        out_shape=jax.ShapeDtypeStruct(queries.shape, jnp.bfloat16),
        in_specs=[pl.BlockSpec(memory_space=pltpu.SMEM)]
        + [pl.BlockSpec(memory_space=pltpu.VMEM)] * 3,
        out_specs=pl.BlockSpec(memory_space=pltpu.VMEM),
        compiler_params=VMEM,
        cost_estimate=small(),
        name="attend",
    )(ids, queries, is_open, kv)


def project_kernel(pieces, context_ref, *refs):
    weights, (mine, sib) = refs[: len(pieces)], refs[len(pieces) :]
    clen = mine.shape[0]
    totals = {}
    for (r, row), weight in zip(pieces, weights):
        term = jnp.dot(
            context_ref[:, row : row + weight.shape[0]],
            weight[...],
            preferred_element_type=jnp.float32,
        )
        totals[r] = term if r not in totals else totals[r] + term
        if row + weight.shape[0] == context_ref.shape[1]:
            block = weight.shape[1]
            rows = totals[r].astype(jnp.bfloat16)
            mine[:, r * block : (r + 1) * block] = rows[:clen]
            sib[:, r * block : (r + 1) * block] = rows[clen:]


def project(context, weights):
    rows, local = context.shape
    pieces, row = [], 0
    for weight in weights:
        pieces.append((row // local, row % local))
        row += weight.shape[0]
    width = row // local * weights[0].shape[1]
    shape = jax.ShapeDtypeStruct((rows // 2, width), jnp.bfloat16)
    return pl.pallas_call(
        functools.partial(project_kernel, pieces),
        out_shape=[shape, shape],
        in_specs=[pl.BlockSpec(memory_space=pltpu.VMEM)] * (1 + len(weights)),
        out_specs=[pl.BlockSpec(memory_space=pltpu.VMEM)] * 2,
        compiler_params=VMEM,
        cost_estimate=small(),
        name="project",
    )(context, *weights)


def finish_kernel(parts, ids, counts, *refs):
    out_ref = refs[-1]
    chunks = (len(refs) - 1) // 3
    block = out_ref.shape[1] // parts
    live = jnp.where(ids[1] < counts[0], 1.0, 0.0)
    r = 0
    for chunk in range(chunks):
        mine, other, passed = refs[3 * chunk : 3 * chunk + 3]
        for start in range(0, mine.shape[1], block):
            columns = slice(start, start + block)
            total = mine[:, columns].astype(jnp.float32) + other[:, columns].astype(jnp.float32)
            total = total + passed[:, columns].astype(jnp.float32)
            target = pl.multiple_of(jnp.bitwise_xor(ids[0], r) * block, block)
            out_ref[:, pl.ds(target, block)] = (total * live).astype(jnp.bfloat16)
            r += 1


def finish(ids, counts, sums, parts, width):
    return pl.pallas_call(
        functools.partial(finish_kernel, parts),
        out_shape=jax.ShapeDtypeStruct((sums[0].shape[0], width), jnp.bfloat16),
        in_specs=[pl.BlockSpec(memory_space=pltpu.SMEM)] * 2
        + [pl.BlockSpec(memory_space=pltpu.VMEM)] * len(sums),
        out_specs=pl.BlockSpec(memory_space=pltpu.VMEM),
        compiler_params=VMEM,
        cost_estimate=small(),
        name="finish",
    )(ids, counts, *sums)


def shards(parts, devices, cand_states, enc_rows, w_query, w_key, w_value, w_out, tile_mask, counts):
    chips = devices // 2
    order = ring_order(chips)
    along = [
        (2 * order[i] + core, 2 * order[(i + 1) % chips] + core)
        for i in range(chips)
        for core in range(2)
    ]
    across = [(c, c ^ 1) for c in range(devices)]

    def to_next(value):
        return lax.ppermute(value, "cand", along)

    def to_sib(value):
        return lax.ppermute(value, "cand", across)

    def flip(value, r):
        return lax.ppermute(value, "prod", [(q, q ^ r) for q in range(parts)])

    ids = jnp.stack([lax.axis_index("prod"), lax.axis_index("cand")]).astype(jnp.int32)

    clen, width = cand_states.shape[2:]
    states = cand_states.reshape(clen, width)
    pairs = [(states, to_sib(states))]
    top = to_next(states[: clen // 2])

    half = w_query.shape[0] // 2
    if parts == 4:
        upper, lower = w_query[:half], w_query[half:]
        first = [flip(upper, 1), flip(lower, 2)]
    else:
        first = [flip(w_query, 1)]

    rows = enc_rows.shape[1]
    block = width // parts
    columns = column_blocks(ids, enc_rows.reshape(rows, width), parts)
    columns = [columns[0]] + [flip(columns[r], r) for r in range(1, parts)]
    tiles = tile_mask.shape[2]
    flags = tile_mask.reshape(1, tiles, 1).astype(jnp.bfloat16)
    flags = jnp.broadcast_to(flags, (FLAG_ROWS, tiles, block // tiles)).reshape(FLAG_ROWS, block)
    piece = jnp.concatenate(columns + [flags], axis=0)
    piece, top, first = lax.optimization_barrier((piece, top, first))
    gathered = lax.all_gather(piece, "cand", axis=0)

    states = jnp.concatenate([top, to_next(states[clen // 2 :])], axis=0)
    pairs.append((states, to_sib(states)))
    for _ in range(2, chips):
        states = to_next(states)
        pairs.append((states, to_sib(states)))
    if parts == 4:
        corner = [flip(first[0], 2), flip(first[1], 1)]
        query_parts = [w_query, first[0], flip(lower, 1), flip(upper, 2), first[1]] + corner
    else:
        query_parts = [w_query, first[0]] + [flip(w_query, r) for r in range(2, parts)]

    query_parts, w_out = lax.optimization_barrier((query_parts, w_out))
    out_parts = [w_out] + [flip(w_out, r) for r in range(1, parts if parts != 4 else 3)]
    if parts == 4:
        half = w_out.shape[0] // 2
        out_parts += [flip(out_parts[1][:half], 2), flip(out_parts[2][half:], 1)]
    out_chunks = [out_parts[: parts // 2], out_parts[parts // 2 :]]

    is_open, *sums = key_value(gathered, w_key, w_value, parts, rows, tiles)
    kv = sums[0]
    for r in range(1, parts):
        kv = kv + flip(sums[r], r).astype(jnp.float32)
    kv = kv.astype(jnp.bfloat16)

    passed = [None] * len(out_chunks)
    for step in list(range(1, chips)) + [0]:
        queries = query(ids, *pairs[step], query_parts, parts)
        context = attend(order, step, ids, queries, is_open, kv)
        last = []
        for chunk, weights in enumerate(out_chunks):
            mine, sib = project(context, weights)
            other = to_sib(sib)
            if step:
                total = mine.astype(jnp.float32) + other.astype(jnp.float32)
                if passed[chunk] is not None:
                    total = total + passed[chunk].astype(jnp.float32)
                passed[chunk] = to_next(total.astype(jnp.bfloat16))
            else:
                last += [mine, other, passed[chunk]]
    return finish(ids, counts, last, parts, width).reshape(cand_states.shape)


def solution(mesh):
    parts, devices = mesh.shape["prod"], mesh.shape["cand"]
    return jax.shard_map(
        functools.partial(shards, parts, devices),
        mesh=mesh,
        in_specs=(
            P("prod", "cand", None, None),
            P("prod", "cand", None),
            P("prod", "cand"),
            P("prod", "cand"),
            P("prod", "cand"),
            P("cand", "prod"),
            P("prod", "cand", None),
            P("prod"),
        ),
        out_specs=P("prod", "cand", None, None),
        check_vma=False,
    )
```

```python
import functools

import jax
import jax.numpy as jnp
from jax import lax
from jax.experimental import pallas as pl
from jax.experimental.pallas import tpu as pltpu
from jax.sharding import PartitionSpec as P

HD = 64
TILE = 128
LANES = 128
FLAG_ROWS = 16
VMEM = pltpu.CompilerParams(vmem_limit_bytes=40 * 1024 * 1024)


def ring_order(chips):
    odd = list(range(1, chips, 2))
    even = list(range(2, chips, 2))
    return [0] + odd + even[::-1]


def small():
    return pl.CostEstimate(flops=1, bytes_accessed=1, transcendentals=0)


def columns_kernel(ids, x_ref, *outs):
    block = outs[0].shape[1]
    for r, out in enumerate(outs):
        source = jnp.bitwise_xor(ids[0], r)
        out[...] = x_ref[:, pl.ds(pl.multiple_of(source * block, block), block)]


def column_blocks(ids, x, parts):
    shape = jax.ShapeDtypeStruct((x.shape[0], x.shape[1] // parts), x.dtype)
    return pl.pallas_call(
        columns_kernel,
        out_shape=[shape] * parts,
        in_specs=[
            pl.BlockSpec(memory_space=pltpu.SMEM),
            pl.BlockSpec(memory_space=pltpu.VMEM),
        ],
        out_specs=[pl.BlockSpec(memory_space=pltpu.VMEM)] * parts,
        compiler_params=VMEM,
        cost_estimate=small(),
        name="columns",
    )(ids, x)


def key_value_kernel(plan, parts, rows, tiles, enc_ref, w_key, w_value, open_ref, *outs):
    slots, height, block = enc_ref.shape
    elen = slots * rows
    encoder = jnp.concatenate([enc_ref[slot, : parts * rows, :] for slot in range(slots)], axis=0)
    for which, weight in enumerate((w_key, w_value)):
        sums = jnp.dot(encoder, weight[...], preferred_element_type=jnp.float32)
        for (kind, places, _), out in zip(plan, outs):
            if kind != which:
                continue
            for index, r in enumerate(places):
                for slot in range(slots):
                    start, target = (slot * parts + r) * rows, index * elen + slot * rows
                    out[target : target + rows, :] = sums[start : start + rows].astype(out.dtype)
    tile = lax.broadcasted_iota(jnp.int32, (1, elen), 1) // TILE
    for slot in range(slots):
        seen = jnp.zeros((1, elen), jnp.float32)
        for t in range(tiles):
            start = t * (block // tiles)
            flag = enc_ref[slot, height - 1 : height, start : start + elen].astype(jnp.float32)
            seen = jnp.where(tile == t, flag, seen)
        open_ref[slot : slot + 1, :] = seen


def key_value(plan, gathered, w_key, w_value, parts, rows, tiles):
    slots, local = gathered.shape[0], w_key.shape[1]
    elen = slots * rows
    return pl.pallas_call(
        functools.partial(key_value_kernel, plan, parts, rows, tiles),
        out_shape=[jax.ShapeDtypeStruct((slots, elen), jnp.float32)]
        + [jax.ShapeDtypeStruct((len(places) * elen, local), kept) for _, places, kept in plan],
        in_specs=[pl.BlockSpec(memory_space=pltpu.VMEM)] * 3,
        out_specs=[pl.BlockSpec(memory_space=pltpu.VMEM)] * (len(plan) + 1),
        compiler_params=pltpu.CompilerParams(vmem_limit_bytes=58 * 1024 * 1024),
        cost_estimate=small(),
        name="key_value",
    )(gathered, w_key, w_value)


def query_kernel(pieces, parts, ids, mine, sib, *refs):
    weights, out_ref = refs[:pieces], refs[pieces]
    clen, width = mine.shape
    block = width // parts
    scales = []
    for ref in (mine, sib):
        values = ref[...].astype(jnp.float32)
        scales.append(lax.rsqrt(jnp.sum(values * values, axis=-1, keepdims=True) / width + 1e-06))
    total, start = None, 0
    for weight in weights:
        depth = weight.shape[0]
        from_prod = jnp.bitwise_xor(ids[0], start // block)
        source = pl.multiple_of(from_prod * block + start % block, LANES)
        rows = jnp.concatenate(
            [
                (ref[:, pl.ds(source, depth)].astype(jnp.float32) * scale).astype(jnp.bfloat16)
                for ref, scale in zip((mine, sib), scales)
            ],
            axis=0,
        )
        term = jnp.dot(rows, weight[...], preferred_element_type=jnp.float32)
        total = term if total is None else total + term
        start += depth
    out_ref[...] = total.astype(jnp.bfloat16)


def query(ids, mine, sib, weights, parts):
    clen = mine.shape[0]
    return pl.pallas_call(
        functools.partial(query_kernel, len(weights), parts),
        out_shape=jax.ShapeDtypeStruct((2 * clen, weights[0].shape[1]), jnp.bfloat16),
        in_specs=[pl.BlockSpec(memory_space=pltpu.SMEM)]
        + [pl.BlockSpec(memory_space=pltpu.VMEM)] * (2 + len(weights)),
        out_specs=pl.BlockSpec(memory_space=pltpu.VMEM),
        compiler_params=VMEM,
        cost_estimate=small(),
        name="query",
    )(ids, mine, sib, *weights)


def attend_kernel(order, step, ids, query_ref, open_ref, key_ref, value_ref, out_ref):
    chips = len(order)
    chip, core = lax.div(ids[1], 2), lax.rem(ids[1], 2)
    source = chip
    if step:
        for place in range(chips):
            source = jnp.where(chip == order[place], order[(place - step) % chips], source)
    who = (2 * source + core, 2 * source + 1 - core)
    clen = query_ref.shape[0] // 2
    elen, local = key_ref.shape
    is_open = (
        jnp.concatenate(
            [jnp.broadcast_to(open_ref[pl.ds(who[i], 1), :], (clen, elen)) for i in range(2)],
            axis=0,
        )
        > 0.5
    )
    lane = lax.broadcasted_iota(jnp.int32, (elen, LANES), 1) // HD
    for pair in range(local // LANES):
        columns = slice(pair * LANES, (pair + 1) * LANES)
        keys, values = key_ref[:, columns], value_ref[:, columns]
        context = None
        for half in range(LANES // HD):
            own = lane == half
            scores = (
                lax.dot_general(
                    query_ref[:, columns],
                    jnp.where(own, keys, jnp.zeros_like(keys)),
                    (((1,), (1,)), ((), ())),
                    preferred_element_type=jnp.float32,
                )
                * 0.125
            )
            scores = jnp.where(is_open, scores, -1e30)
            top = jnp.max(scores, axis=-1, keepdims=True)
            grown = jnp.exp(scores - top)
            probs = (grown / jnp.sum(grown, axis=-1, keepdims=True)).astype(jnp.bfloat16)
            term = jnp.dot(
                probs,
                jnp.where(own, values, jnp.zeros_like(values)),
                preferred_element_type=jnp.float32,
            )
            context = term if context is None else context + term
        out_ref[:, columns] = context.astype(jnp.bfloat16)


def attend(order, step, ids, queries, is_open, keys, values):
    return pl.pallas_call(
        functools.partial(attend_kernel, order, step),
        out_shape=jax.ShapeDtypeStruct(queries.shape, jnp.bfloat16),
        in_specs=[pl.BlockSpec(memory_space=pltpu.SMEM)]
        + [pl.BlockSpec(memory_space=pltpu.VMEM)] * 4,
        out_specs=pl.BlockSpec(memory_space=pltpu.VMEM),
        compiler_params=VMEM,
        cost_estimate=small(),
        name="attend",
    )(ids, queries, is_open, keys, values)


def project_kernel(pieces, context_ref, *refs):
    weights, (mine, sib) = refs[: len(pieces)], refs[len(pieces) :]
    clen = mine.shape[0]
    totals = {}
    for (r, row), weight in zip(pieces, weights):
        term = jnp.dot(
            context_ref[:, row : row + weight.shape[0]],
            weight[...],
            preferred_element_type=jnp.float32,
        )
        totals[r] = term if r not in totals else totals[r] + term
        if row + weight.shape[0] == context_ref.shape[1]:
            block = weight.shape[1]
            rows = totals[r].astype(jnp.bfloat16)
            mine[:, r * block : (r + 1) * block] = rows[:clen]
            sib[:, r * block : (r + 1) * block] = rows[clen:]


def project(context, weights):
    rows, local = context.shape
    pieces, row = [], 0
    for weight in weights:
        pieces.append((row // local, row % local))
        row += weight.shape[0]
    width = row // local * weights[0].shape[1]
    shape = jax.ShapeDtypeStruct((rows // 2, width), jnp.bfloat16)
    return pl.pallas_call(
        functools.partial(project_kernel, pieces),
        out_shape=[shape, shape],
        in_specs=[pl.BlockSpec(memory_space=pltpu.VMEM)] * (1 + len(weights)),
        out_specs=[pl.BlockSpec(memory_space=pltpu.VMEM)] * 2,
        compiler_params=VMEM,
        cost_estimate=small(),
        name="project",
    )(context, *weights)


def finish_kernel(parts, ids, counts, *refs):
    out_ref = refs[-1]
    chunks = (len(refs) - 1) // 3
    block = out_ref.shape[1] // parts
    live = jnp.where(ids[1] < counts[0], 1.0, 0.0)
    r = 0
    for chunk in range(chunks):
        mine, other, passed = refs[3 * chunk : 3 * chunk + 3]
        for start in range(0, mine.shape[1], block):
            columns = slice(start, start + block)
            total = mine[:, columns].astype(jnp.float32) + other[:, columns].astype(jnp.float32)
            total = total + passed[:, columns].astype(jnp.float32)
            target = pl.multiple_of(jnp.bitwise_xor(ids[0], r) * block, block)
            out_ref[:, pl.ds(target, block)] = (total * live).astype(jnp.bfloat16)
            r += 1


def finish(ids, counts, sums, parts, width):
    return pl.pallas_call(
        functools.partial(finish_kernel, parts),
        out_shape=jax.ShapeDtypeStruct((sums[0].shape[0], width), jnp.bfloat16),
        in_specs=[pl.BlockSpec(memory_space=pltpu.SMEM)] * 2
        + [pl.BlockSpec(memory_space=pltpu.VMEM)] * len(sums),
        out_specs=pl.BlockSpec(memory_space=pltpu.VMEM),
        compiler_params=VMEM,
        cost_estimate=small(),
        name="finish",
    )(ids, counts, *sums)


def shards(parts, devices, cand_states, enc_rows, w_query, w_key, w_value, w_out, tile_mask, counts):
    chips = devices // 2
    order = ring_order(chips)
    along = [
        (2 * order[i] + core, 2 * order[(i + 1) % chips] + core)
        for i in range(chips)
        for core in range(2)
    ]
    across = [(c, c ^ 1) for c in range(devices)]

    def to_next(value):
        return lax.ppermute(value, "cand", along)

    def to_sib(value):
        return lax.ppermute(value, "cand", across)

    def flip(value, r):
        return lax.ppermute(value, "prod", [(q, q ^ r) for q in range(parts)])

    ids = jnp.stack([lax.axis_index("prod"), lax.axis_index("cand")]).astype(jnp.int32)

    clen, width = cand_states.shape[2:]
    states = cand_states.reshape(clen, width)
    pairs = [(states, to_sib(states))]
    states = to_next(states)

    def corner(weight, first, second):
        half = weight.shape[0] // 2
        return [flip(first[:half], 2), flip(second[half:], 1)]

    query_parts = [w_query] + [flip(w_query, r) for r in range(1, min(parts, 3))]

    rows = enc_rows.shape[1]
    block = width // parts
    columns = column_blocks(ids, enc_rows.reshape(rows, width), parts)
    columns = [columns[0]] + [flip(columns[r], r) for r in range(1, parts)]
    tiles = tile_mask.shape[2]
    flags = tile_mask.reshape(1, tiles, 1).astype(jnp.bfloat16)
    flags = jnp.broadcast_to(flags, (FLAG_ROWS, tiles, block // tiles)).reshape(FLAG_ROWS, block)
    piece = jnp.concatenate(columns + [flags], axis=0)
    piece, states, query_parts = lax.optimization_barrier((piece, states, query_parts))
    gathered = lax.all_gather(piece, "cand", axis=0)

    pairs.append((states, to_sib(states)))
    for _ in range(2, chips):
        states = to_next(states)
        pairs.append((states, to_sib(states)))
    if parts == 4:
        query_parts += corner(*query_parts)
    else:
        query_parts += [flip(w_query, r) for r in range(3, parts)]

    query_parts, w_out = lax.optimization_barrier((query_parts, w_out))
    out_parts = [w_out] + [flip(w_out, r) for r in range(1, parts if parts != 4 else 3)]
    if parts == 4:
        out_parts += corner(*out_parts)
    out_chunks = [out_parts[: parts // 2], out_parts[parts // 2 :]]

    f32, bf16 = jnp.float32, jnp.bfloat16
    elen = devices * rows
    if parts == 4:
        plan = [(0, (0,), f32), (0, (2,), f32), (0, (1, 3), bf16)]
        plan += [(1, (0,), f32), (1, (1,), f32), (1, (2, 3), bf16)]
    else:
        plan = [(which, (r,), bf16 if r else f32) for which in range(2) for r in range(parts)]
    is_open, *sums = key_value(plan, gathered, w_key, w_value, parts, rows, tiles)
    if parts == 4:
        (key, key_far, key_sent), (value, value_far, value_sent) = sums[:3], sums[3:]
        came = lax.optimization_barrier((flip(key_sent, 1), flip(value_sent, 2)))
        came = [rows_in.astype(f32) for rows_in in came]
        far = [(key_far + came[0][elen:]).astype(bf16), (value_far + came[1][elen:]).astype(bf16)]
        far = lax.optimization_barrier((flip(far[0], 2), flip(far[1], 1)))
        projected = [
            (own + near[:elen] + last.astype(f32)).astype(bf16)
            for own, near, last in zip((key, value), came, far)
        ]
    else:
        projected = []
        for own, *others in (sums[:parts], sums[parts:]):
            for r in range(1, parts):
                own = own + flip(others[r - 1], r).astype(f32)
            projected.append(own.astype(bf16))

    steps = list(range(1, chips)) + [0]
    passed = [None] * len(out_chunks)
    queries = query(ids, *pairs[steps[0]], query_parts, parts)
    for index, step in enumerate(steps):
        context = attend(order, step, ids, queries, is_open, *projected)
        sums = []
        for weights in out_chunks:
            mine, sib = project(context, weights)
            sums.append((mine, to_sib(sib)))
        if not step:
            break
        totals = []
        for chunk, (mine, other) in enumerate(sums):
            total = mine.astype(f32) + other.astype(f32)
            if passed[chunk] is not None:
                total = total + passed[chunk].astype(f32)
            totals.append(total.astype(bf16))
        queries = query(ids, *pairs[steps[index + 1]], query_parts, parts)
        if not index:
            totals, queries = lax.optimization_barrier((totals, queries))
        passed = [to_next(total) for total in totals]
    last = [part for (mine, other), came in zip(sums, passed) for part in (mine, other, came)]
    return finish(ids, counts, last, parts, width).reshape(cand_states.shape)


def solution(mesh):
    parts, devices = mesh.shape["prod"], mesh.shape["cand"]
    return jax.shard_map(
        functools.partial(shards, parts, devices),
        mesh=mesh,
        in_specs=(
            P("prod", "cand", None, None),
            P("prod", "cand", None),
            P("prod", "cand"),
            P("prod", "cand"),
            P("prod", "cand"),
            P("cand", "prod"),
            P("prod", "cand", None),
            P("prod"),
        ),
        out_specs=P("prod", "cand", None, None),
        check_vma=False,
    )
```

```python
import functools

import jax
import jax.numpy as jnp
from jax import lax
from jax.experimental import pallas as pl
from jax.experimental.pallas import tpu as pltpu
from jax.sharding import PartitionSpec as P

HD = 64
TILE = 128
LANES = 128
FLAG_ROWS = 16
VMEM = pltpu.CompilerParams(vmem_limit_bytes=40 * 1024 * 1024)


def ring_order(chips):
    odd = list(range(1, chips, 2))
    even = list(range(2, chips, 2))
    return [0] + odd + even[::-1]


def small():
    return pl.CostEstimate(flops=1, bytes_accessed=1, transcendentals=0)


def prepare_kernel(parts, ids, x_ref, states_ref, *outs):
    blocks, (top, rest) = outs[:parts], outs[parts:]
    block = blocks[0].shape[1]
    for r, out in enumerate(blocks):
        source = jnp.bitwise_xor(ids[0], r)
        out[...] = x_ref[:, pl.ds(pl.multiple_of(source * block, block), block)]
    cut = top.shape[0]
    top[...] = states_ref[:cut, :]
    rest[...] = states_ref[cut:, :]


def prepare(ids, x, states, parts, cut):
    rows, width = x.shape
    clen = states.shape[0]
    return pl.pallas_call(
        functools.partial(prepare_kernel, parts),
        out_shape=[jax.ShapeDtypeStruct((rows, width // parts), x.dtype)] * parts
        + [jax.ShapeDtypeStruct((size, width), x.dtype) for size in (cut, clen - cut)],
        in_specs=[pl.BlockSpec(memory_space=pltpu.SMEM)]
        + [pl.BlockSpec(memory_space=pltpu.VMEM)] * 2,
        out_specs=[pl.BlockSpec(memory_space=pltpu.VMEM)] * (parts + 2),
        compiler_params=VMEM,
        cost_estimate=small(),
        name="prepare",
    )(ids, x, states)


def key_value_kernel(plan, parts, rows, tiles, enc_ref, w_key, w_value, open_ref, *outs):
    slots, height, block = enc_ref.shape
    elen = slots * rows
    encoder = jnp.concatenate([enc_ref[slot, : parts * rows, :] for slot in range(slots)], axis=0)
    for which, weight in enumerate((w_key, w_value)):
        sums = jnp.dot(encoder, weight[...], preferred_element_type=jnp.float32)
        for (kind, places, _), out in zip(plan, outs):
            if kind != which:
                continue
            for index, r in enumerate(places):
                for slot in range(slots):
                    start, target = (slot * parts + r) * rows, index * elen + slot * rows
                    out[target : target + rows, :] = sums[start : start + rows].astype(out.dtype)
    tile = lax.broadcasted_iota(jnp.int32, (1, elen), 1) // TILE
    for slot in range(slots):
        seen = jnp.zeros((1, elen), jnp.float32)
        for t in range(tiles):
            start = t * (block // tiles)
            flag = enc_ref[slot, height - 1 : height, start : start + elen].astype(jnp.float32)
            seen = jnp.where(tile == t, flag, seen)
        open_ref[slot : slot + 1, :] = seen


def key_value(plan, gathered, w_key, w_value, parts, rows, tiles):
    slots, local = gathered.shape[0], w_key.shape[1]
    elen = slots * rows
    return pl.pallas_call(
        functools.partial(key_value_kernel, plan, parts, rows, tiles),
        out_shape=[jax.ShapeDtypeStruct((slots, elen), jnp.float32)]
        + [jax.ShapeDtypeStruct((len(places) * elen, local), kept) for _, places, kept in plan],
        in_specs=[pl.BlockSpec(memory_space=pltpu.VMEM)] * 3,
        out_specs=[pl.BlockSpec(memory_space=pltpu.VMEM)] * (len(plan) + 1),
        compiler_params=pltpu.CompilerParams(vmem_limit_bytes=58 * 1024 * 1024),
        cost_estimate=small(),
        name="key_value",
    )(gathered, w_key, w_value)


def query_kernel(pieces, parts, ids, mine, sib, *refs):
    weights, out_ref = refs[:pieces], refs[pieces]
    clen, width = mine.shape
    block = width // parts
    scales = []
    for ref in (mine, sib):
        values = ref[...].astype(jnp.float32)
        scales.append(lax.rsqrt(jnp.sum(values * values, axis=-1, keepdims=True) / width + 1e-06))
    total, start = None, 0
    for weight in weights:
        depth = weight.shape[0]
        from_prod = jnp.bitwise_xor(ids[0], start // block)
        source = pl.multiple_of(from_prod * block + start % block, LANES)
        rows = jnp.concatenate(
            [
                (ref[:, pl.ds(source, depth)].astype(jnp.float32) * scale).astype(jnp.bfloat16)
                for ref, scale in zip((mine, sib), scales)
            ],
            axis=0,
        )
        term = jnp.dot(rows, weight[...], preferred_element_type=jnp.float32)
        total = term if total is None else total + term
        start += depth
    out_ref[...] = total.astype(jnp.bfloat16)


def query(ids, mine, sib, weights, parts):
    clen = mine.shape[0]
    return pl.pallas_call(
        functools.partial(query_kernel, len(weights), parts),
        out_shape=jax.ShapeDtypeStruct((2 * clen, weights[0].shape[1]), jnp.bfloat16),
        in_specs=[pl.BlockSpec(memory_space=pltpu.SMEM)]
        + [pl.BlockSpec(memory_space=pltpu.VMEM)] * (2 + len(weights)),
        out_specs=pl.BlockSpec(memory_space=pltpu.VMEM),
        compiler_params=VMEM,
        cost_estimate=small(),
        name="query",
    )(ids, mine, sib, *weights)


def attend_kernel(order, step, ids, query_ref, open_ref, key_ref, value_ref, out_ref):
    chips = len(order)
    chip, core = lax.div(ids[1], 2), lax.rem(ids[1], 2)
    source = chip
    if step:
        for place in range(chips):
            source = jnp.where(chip == order[place], order[(place - step) % chips], source)
    who = (2 * source + core, 2 * source + 1 - core)
    clen = query_ref.shape[0] // 2
    elen, local = key_ref.shape
    is_open = (
        jnp.concatenate(
            [jnp.broadcast_to(open_ref[pl.ds(who[i], 1), :], (clen, elen)) for i in range(2)],
            axis=0,
        )
        > 0.5
    )
    lane = lax.broadcasted_iota(jnp.int32, (elen, LANES), 1) // HD
    for pair in range(local // LANES):
        columns = slice(pair * LANES, (pair + 1) * LANES)
        keys, values = key_ref[:, columns], value_ref[:, columns]
        context = None
        for half in range(LANES // HD):
            own = lane == half
            scores = (
                lax.dot_general(
                    query_ref[:, columns],
                    jnp.where(own, keys, jnp.zeros_like(keys)),
                    (((1,), (1,)), ((), ())),
                    preferred_element_type=jnp.float32,
                )
                * 0.125
            )
            scores = jnp.where(is_open, scores, -1e30)
            top = jnp.max(scores, axis=-1, keepdims=True)
            grown = jnp.exp(scores - top)
            probs = (grown / jnp.sum(grown, axis=-1, keepdims=True)).astype(jnp.bfloat16)
            term = jnp.dot(
                probs,
                jnp.where(own, values, jnp.zeros_like(values)),
                preferred_element_type=jnp.float32,
            )
            context = term if context is None else context + term
        out_ref[:, columns] = context.astype(jnp.bfloat16)


def attend(order, step, ids, queries, is_open, keys, values):
    return pl.pallas_call(
        functools.partial(attend_kernel, order, step),
        out_shape=jax.ShapeDtypeStruct(queries.shape, jnp.bfloat16),
        in_specs=[pl.BlockSpec(memory_space=pltpu.SMEM)]
        + [pl.BlockSpec(memory_space=pltpu.VMEM)] * 4,
        out_specs=pl.BlockSpec(memory_space=pltpu.VMEM),
        compiler_params=VMEM,
        cost_estimate=small(),
        name="attend",
    )(ids, queries, is_open, keys, values)


def project_kernel(pieces, context_ref, *refs):
    weights, (mine, sib) = refs[: len(pieces)], refs[len(pieces) :]
    clen = mine.shape[0]
    totals = {}
    for (r, row), weight in zip(pieces, weights):
        term = jnp.dot(
            context_ref[:, row : row + weight.shape[0]],
            weight[...],
            preferred_element_type=jnp.float32,
        )
        totals[r] = term if r not in totals else totals[r] + term
        if row + weight.shape[0] == context_ref.shape[1]:
            block = weight.shape[1]
            rows = totals[r].astype(jnp.bfloat16)
            mine[:, r * block : (r + 1) * block] = rows[:clen]
            sib[:, r * block : (r + 1) * block] = rows[clen:]


def project(context, weights):
    rows, local = context.shape
    pieces, row = [], 0
    for weight in weights:
        pieces.append((row // local, row % local))
        row += weight.shape[0]
    width = row // local * weights[0].shape[1]
    shape = jax.ShapeDtypeStruct((rows // 2, width), jnp.bfloat16)
    return pl.pallas_call(
        functools.partial(project_kernel, pieces),
        out_shape=[shape, shape],
        in_specs=[pl.BlockSpec(memory_space=pltpu.VMEM)] * (1 + len(weights)),
        out_specs=[pl.BlockSpec(memory_space=pltpu.VMEM)] * 2,
        compiler_params=VMEM,
        cost_estimate=small(),
        name="project",
    )(context, *weights)


def finish_kernel(parts, ids, counts, *refs):
    out_ref = refs[-1]
    chunks = (len(refs) - 1) // 3
    block = out_ref.shape[1] // parts
    live = jnp.where(ids[1] < counts[0], 1.0, 0.0)
    r = 0
    for chunk in range(chunks):
        mine, other, passed = refs[3 * chunk : 3 * chunk + 3]
        for start in range(0, mine.shape[1], block):
            columns = slice(start, start + block)
            total = mine[:, columns].astype(jnp.float32) + other[:, columns].astype(jnp.float32)
            total = total + passed[:, columns].astype(jnp.float32)
            target = pl.multiple_of(jnp.bitwise_xor(ids[0], r) * block, block)
            out_ref[:, pl.ds(target, block)] = (total * live).astype(jnp.bfloat16)
            r += 1


def finish(ids, counts, sums, parts, width):
    return pl.pallas_call(
        functools.partial(finish_kernel, parts),
        out_shape=jax.ShapeDtypeStruct((sums[0].shape[0], width), jnp.bfloat16),
        in_specs=[pl.BlockSpec(memory_space=pltpu.SMEM)] * 2
        + [pl.BlockSpec(memory_space=pltpu.VMEM)] * len(sums),
        out_specs=pl.BlockSpec(memory_space=pltpu.VMEM),
        compiler_params=VMEM,
        cost_estimate=small(),
        name="finish",
    )(ids, counts, *sums)


def shards(parts, devices, cand_states, enc_rows, w_query, w_key, w_value, w_out, tile_mask, counts):
    chips = devices // 2
    order = ring_order(chips)
    along = [
        (2 * order[i] + core, 2 * order[(i + 1) % chips] + core)
        for i in range(chips)
        for core in range(2)
    ]
    across = [(c, c ^ 1) for c in range(devices)]

    def to_next(value):
        return lax.ppermute(value, "cand", along)

    def to_sib(value):
        return lax.ppermute(value, "cand", across)

    def flip(value, r):
        return lax.ppermute(value, "prod", [(q, q ^ r) for q in range(parts)])

    ids = jnp.stack([lax.axis_index("prod"), lax.axis_index("cand")]).astype(jnp.int32)

    clen, width = cand_states.shape[2:]
    states = cand_states.reshape(clen, width)
    rows = enc_rows.shape[1]
    block = width // parts
    *columns, top, rest = prepare(ids, enc_rows.reshape(rows, width), states, parts, clen // 4)
    columns = [columns[0]] + [flip(columns[r], r) for r in range(1, parts)]
    tiles = tile_mask.shape[2]
    flags = tile_mask.reshape(1, tiles, 1).astype(jnp.bfloat16)
    flags = jnp.broadcast_to(flags, (FLAG_ROWS, tiles, block // tiles)).reshape(FLAG_ROWS, block)
    piece = jnp.concatenate(columns + [flags], axis=0)
    piece, top = lax.optimization_barrier((piece, to_next(top)))
    gathered = lax.all_gather(piece, "cand", axis=0)

    def corner(weight, first, second):
        half = weight.shape[0] // 2
        return [flip(first[:half], 2), flip(second[half:], 1)]

    query_parts = [w_query] + [flip(w_query, r) for r in range(1, min(parts, 3))]
    if parts == 4:
        query_parts += corner(*query_parts)
    else:
        query_parts += [flip(w_query, r) for r in range(3, parts)]

    pairs = [(states, to_sib(states))]
    states = jnp.concatenate([top, to_next(rest)], axis=0)
    gathered, states, query_parts, w_out = lax.optimization_barrier(
        (gathered, states, query_parts, w_out)
    )
    pairs.append((states, to_sib(states)))
    states = to_next(states)
    out_parts = [w_out] + [flip(w_out, r) for r in range(1, parts if parts != 4 else 3)]

    f32, bf16 = jnp.float32, jnp.bfloat16
    elen = devices * rows
    if parts == 4:
        plan = [(0, (0,), f32), (0, (2,), f32), (0, (1, 3), bf16)]
        plan += [(1, (0,), f32), (1, (1,), f32), (1, (2, 3), bf16)]
    else:
        plan = [(which, (r,), bf16 if r else f32) for which in range(2) for r in range(parts)]
    is_open, *sums = key_value(plan, gathered, w_key, w_value, parts, rows, tiles)
    sums, out_parts, states = lax.optimization_barrier((sums, out_parts, states))
    pairs.append((states, to_sib(states)))
    top = to_next(states[: clen // 2])
    if parts == 4:
        (key, key_far, key_sent), (value, value_far, value_sent) = sums[:3], sums[3:]
        came = [flip(key_sent, 1), flip(value_sent, 2)]
        came, out_parts, top = lax.optimization_barrier((came, out_parts, top))
        came = [rows_in.astype(f32) for rows_in in came]
        far = [(key_far + came[0][elen:]).astype(bf16), (value_far + came[1][elen:]).astype(bf16)]
        far = lax.optimization_barrier((flip(far[0], 2), flip(far[1], 1)))
        projected = [
            (own + near[:elen] + last.astype(f32)).astype(bf16)
            for own, near, last in zip((key, value), came, far)
        ]
    else:
        projected = []
        for own, *others in (sums[:parts], sums[parts:]):
            for r in range(1, parts):
                own = own + flip(others[r - 1], r).astype(f32)
            projected.append(own.astype(bf16))
    if parts == 4:
        out_parts += corner(*out_parts)
    out_chunks = [out_parts[: parts // 2], out_parts[parts // 2 :]]

    states = jnp.concatenate([top, to_next(states[clen // 2 :])], axis=0)
    for hop in range(3, chips):
        pairs.append((states, to_sib(states)))
        if hop < chips - 1:
            states = to_next(states)

    steps = list(range(1, chips)) + [0]
    passed = [None] * len(out_chunks)
    queries = query(ids, *pairs[steps[0]], query_parts, parts)
    for index, step in enumerate(steps):
        context = attend(order, step, ids, queries, is_open, *projected)
        sums = []
        for weights in out_chunks:
            mine, sib = project(context, weights)
            sums.append((mine, to_sib(sib)))
        if not step:
            break
        totals = []
        for chunk, (mine, other) in enumerate(sums):
            total = mine.astype(f32) + other.astype(f32)
            if passed[chunk] is not None:
                total = total + passed[chunk].astype(f32)
            totals.append(total.astype(bf16))
        queries = query(ids, *pairs[steps[index + 1]], query_parts, parts)
        if not index:
            totals, queries = lax.optimization_barrier((totals, queries))
        passed = [to_next(total) for total in totals]
    last = [part for (mine, other), came in zip(sums, passed) for part in (mine, other, came)]
    return finish(ids, counts, last, parts, width).reshape(cand_states.shape)


def solution(mesh):
    parts, devices = mesh.shape["prod"], mesh.shape["cand"]
    return jax.shard_map(
        functools.partial(shards, parts, devices),
        mesh=mesh,
        in_specs=(
            P("prod", "cand", None, None),
            P("prod", "cand", None),
            P("prod", "cand"),
            P("prod", "cand"),
            P("prod", "cand"),
            P("cand", "prod"),
            P("prod", "cand", None),
            P("prod"),
        ),
        out_specs=P("prod", "cand", None, None),
        check_vma=False,
    )
```

```python
import functools

import jax
import jax.numpy as jnp
from jax import lax
from jax.experimental import pallas as pl
from jax.experimental.pallas import tpu as pltpu
from jax.sharding import PartitionSpec as P

HD = 64
TILE = 128
LANES = 128
FLAG_ROWS = 16
VMEM = pltpu.CompilerParams(vmem_limit_bytes=40 * 1024 * 1024)


def ring_order(chips):
    odd = list(range(1, chips, 2))
    even = list(range(2, chips, 2))
    return [0] + odd + even[::-1]


def small():
    return pl.CostEstimate(flops=1, bytes_accessed=1, transcendentals=0)


def columns_kernel(ids, x_ref, *outs):
    block = outs[0].shape[1]
    for r, out in enumerate(outs):
        source = jnp.bitwise_xor(ids[0], r)
        out[...] = x_ref[:, pl.ds(pl.multiple_of(source * block, block), block)]


def column_blocks(ids, x, parts):
    shape = jax.ShapeDtypeStruct((x.shape[0], x.shape[1] // parts), x.dtype)
    return pl.pallas_call(
        columns_kernel,
        out_shape=[shape] * parts,
        in_specs=[
            pl.BlockSpec(memory_space=pltpu.SMEM),
            pl.BlockSpec(memory_space=pltpu.VMEM),
        ],
        out_specs=[pl.BlockSpec(memory_space=pltpu.VMEM)] * parts,
        compiler_params=VMEM,
        cost_estimate=small(),
        name="columns",
    )(ids, x)


def key_value_kernel(plan, parts, rows, tiles, enc_ref, w_key, w_value, open_ref, *outs):
    slots, height, block = enc_ref.shape
    elen = slots * rows
    encoder = jnp.concatenate([enc_ref[slot, : parts * rows, :] for slot in range(slots)], axis=0)
    for which, weight in enumerate((w_key, w_value)):
        sums = jnp.dot(encoder, weight[...], preferred_element_type=jnp.float32)
        for (kind, places, _), out in zip(plan, outs):
            if kind != which:
                continue
            for index, r in enumerate(places):
                for slot in range(slots):
                    start, target = (slot * parts + r) * rows, index * elen + slot * rows
                    out[target : target + rows, :] = sums[start : start + rows].astype(out.dtype)
    tile = lax.broadcasted_iota(jnp.int32, (1, elen), 1) // TILE
    for slot in range(slots):
        seen = jnp.zeros((1, elen), jnp.float32)
        for t in range(tiles):
            start = t * (block // tiles)
            flag = enc_ref[slot, height - 1 : height, start : start + elen].astype(jnp.float32)
            seen = jnp.where(tile == t, flag, seen)
        open_ref[slot : slot + 1, :] = seen


def key_value(plan, gathered, w_key, w_value, parts, rows, tiles):
    slots, local = gathered.shape[0], w_key.shape[1]
    elen = slots * rows
    return pl.pallas_call(
        functools.partial(key_value_kernel, plan, parts, rows, tiles),
        out_shape=[jax.ShapeDtypeStruct((slots, elen), jnp.float32)]
        + [jax.ShapeDtypeStruct((len(places) * elen, local), kept) for _, places, kept in plan],
        in_specs=[pl.BlockSpec(memory_space=pltpu.VMEM)] * 3,
        out_specs=[pl.BlockSpec(memory_space=pltpu.VMEM)] * (len(plan) + 1),
        compiler_params=pltpu.CompilerParams(vmem_limit_bytes=58 * 1024 * 1024),
        cost_estimate=small(),
        name="key_value",
    )(gathered, w_key, w_value)


def query_kernel(pieces, parts, ids, mine, sib, *refs):
    weights, out_ref = refs[:pieces], refs[pieces]
    clen, width = mine.shape
    block = width // parts
    scales = []
    for ref in (mine, sib):
        values = ref[...].astype(jnp.float32)
        scales.append(lax.rsqrt(jnp.sum(values * values, axis=-1, keepdims=True) / width + 1e-06))
    total, start = None, 0
    for weight in weights:
        depth = weight.shape[0]
        from_prod = jnp.bitwise_xor(ids[0], start // block)
        source = pl.multiple_of(from_prod * block + start % block, LANES)
        rows = jnp.concatenate(
            [
                (ref[:, pl.ds(source, depth)].astype(jnp.float32) * scale).astype(jnp.bfloat16)
                for ref, scale in zip((mine, sib), scales)
            ],
            axis=0,
        )
        term = jnp.dot(rows, weight[...], preferred_element_type=jnp.float32)
        total = term if total is None else total + term
        start += depth
    out_ref[...] = total.astype(jnp.bfloat16)


def query(ids, mine, sib, weights, parts):
    clen = mine.shape[0]
    return pl.pallas_call(
        functools.partial(query_kernel, len(weights), parts),
        out_shape=jax.ShapeDtypeStruct((2 * clen, weights[0].shape[1]), jnp.bfloat16),
        in_specs=[pl.BlockSpec(memory_space=pltpu.SMEM)]
        + [pl.BlockSpec(memory_space=pltpu.VMEM)] * (2 + len(weights)),
        out_specs=pl.BlockSpec(memory_space=pltpu.VMEM),
        compiler_params=VMEM,
        cost_estimate=small(),
        name="query",
    )(ids, mine, sib, *weights)


def attend_kernel(order, step, ids, query_ref, open_ref, key_ref, value_ref, out_ref):
    chips = len(order)
    chip, core = lax.div(ids[1], 2), lax.rem(ids[1], 2)
    source = chip
    if step:
        for place in range(chips):
            source = jnp.where(chip == order[place], order[(place - step) % chips], source)
    who = (2 * source + core, 2 * source + 1 - core)
    clen = query_ref.shape[0] // 2
    elen, local = key_ref.shape
    is_open = (
        jnp.concatenate(
            [jnp.broadcast_to(open_ref[pl.ds(who[i], 1), :], (clen, elen)) for i in range(2)],
            axis=0,
        )
        > 0.5
    )
    lane = lax.broadcasted_iota(jnp.int32, (elen, LANES), 1) // HD
    for pair in range(local // LANES):
        columns = slice(pair * LANES, (pair + 1) * LANES)
        keys, values = key_ref[:, columns], value_ref[:, columns]
        context = None
        for half in range(LANES // HD):
            own = lane == half
            scores = (
                lax.dot_general(
                    query_ref[:, columns],
                    jnp.where(own, keys, jnp.zeros_like(keys)),
                    (((1,), (1,)), ((), ())),
                    preferred_element_type=jnp.float32,
                )
                * 0.125
            )
            scores = jnp.where(is_open, scores, -1e30)
            top = jnp.max(scores, axis=-1, keepdims=True)
            grown = jnp.exp(scores - top)
            probs = (grown / jnp.sum(grown, axis=-1, keepdims=True)).astype(jnp.bfloat16)
            term = jnp.dot(
                probs,
                jnp.where(own, values, jnp.zeros_like(values)),
                preferred_element_type=jnp.float32,
            )
            context = term if context is None else context + term
        out_ref[:, columns] = context.astype(jnp.bfloat16)


def attend(order, step, ids, queries, is_open, keys, values):
    return pl.pallas_call(
        functools.partial(attend_kernel, order, step),
        out_shape=jax.ShapeDtypeStruct(queries.shape, jnp.bfloat16),
        in_specs=[pl.BlockSpec(memory_space=pltpu.SMEM)]
        + [pl.BlockSpec(memory_space=pltpu.VMEM)] * 4,
        out_specs=pl.BlockSpec(memory_space=pltpu.VMEM),
        compiler_params=VMEM,
        cost_estimate=small(),
        name="attend",
    )(ids, queries, is_open, keys, values)


def project_kernel(pieces, context_ref, *refs):
    weights, (mine, sib) = refs[: len(pieces)], refs[len(pieces) :]
    clen = mine.shape[0]
    totals = {}
    for (r, row), weight in zip(pieces, weights):
        term = jnp.dot(
            context_ref[:, row : row + weight.shape[0]],
            weight[...],
            preferred_element_type=jnp.float32,
        )
        totals[r] = term if r not in totals else totals[r] + term
        if row + weight.shape[0] == context_ref.shape[1]:
            block = weight.shape[1]
            rows = totals[r].astype(jnp.bfloat16)
            mine[:, r * block : (r + 1) * block] = rows[:clen]
            sib[:, r * block : (r + 1) * block] = rows[clen:]


def project(context, weights):
    rows, local = context.shape
    pieces, row = [], 0
    for weight in weights:
        pieces.append((row // local, row % local))
        row += weight.shape[0]
    width = row // local * weights[0].shape[1]
    shape = jax.ShapeDtypeStruct((rows // 2, width), jnp.bfloat16)
    return pl.pallas_call(
        functools.partial(project_kernel, pieces),
        out_shape=[shape, shape],
        in_specs=[pl.BlockSpec(memory_space=pltpu.VMEM)] * (1 + len(weights)),
        out_specs=[pl.BlockSpec(memory_space=pltpu.VMEM)] * 2,
        compiler_params=VMEM,
        cost_estimate=small(),
        name="project",
    )(context, *weights)


def finish_kernel(parts, ids, counts, *refs):
    out_ref = refs[-1]
    chunks = (len(refs) - 1) // 3
    block = out_ref.shape[1] // parts
    live = jnp.where(ids[1] < counts[0], 1.0, 0.0)
    r = 0
    for chunk in range(chunks):
        mine, other, passed = refs[3 * chunk : 3 * chunk + 3]
        for start in range(0, mine.shape[1], block):
            columns = slice(start, start + block)
            total = mine[:, columns].astype(jnp.float32) + other[:, columns].astype(jnp.float32)
            total = total + passed[:, columns].astype(jnp.float32)
            target = pl.multiple_of(jnp.bitwise_xor(ids[0], r) * block, block)
            out_ref[:, pl.ds(target, block)] = (total * live).astype(jnp.bfloat16)
            r += 1


def finish(ids, counts, sums, parts, width):
    return pl.pallas_call(
        functools.partial(finish_kernel, parts),
        out_shape=jax.ShapeDtypeStruct((sums[0].shape[0], width), jnp.bfloat16),
        in_specs=[pl.BlockSpec(memory_space=pltpu.SMEM)] * 2
        + [pl.BlockSpec(memory_space=pltpu.VMEM)] * len(sums),
        out_specs=pl.BlockSpec(memory_space=pltpu.VMEM),
        compiler_params=VMEM,
        cost_estimate=small(),
        name="finish",
    )(ids, counts, *sums)


def shards(parts, devices, cand_states, enc_rows, w_query, w_key, w_value, w_out, tile_mask, counts):
    chips = devices // 2
    order = ring_order(chips)
    along = [
        (2 * order[i] + core, 2 * order[(i + 1) % chips] + core)
        for i in range(chips)
        for core in range(2)
    ]
    across = [(c, c ^ 1) for c in range(devices)]

    def to_next(value):
        return lax.ppermute(value, "cand", along)

    def to_sib(value):
        return lax.ppermute(value, "cand", across)

    def flip(value, r):
        return lax.ppermute(value, "prod", [(q, q ^ r) for q in range(parts)])

    ids = jnp.stack([lax.axis_index("prod"), lax.axis_index("cand")]).astype(jnp.int32)

    clen, width = cand_states.shape[2:]
    states = cand_states.reshape(clen, width)
    pairs = [(states, to_sib(states))]
    states = to_next(states)

    def corner(weight, first, second):
        half = weight.shape[0] // 2
        return [flip(first[:half], 2), flip(second[half:], 1)]

    if parts == 4:
        half = w_query.shape[0] // 2
        upper, lower = w_query[:half], w_query[half:]
        ahead = [flip(upper, 1), flip(lower, 2)]
    else:
        ahead = [flip(w_query, 1)]

    rows = enc_rows.shape[1]
    block = width // parts
    encoder, pairs[0] = lax.optimization_barrier((enc_rows.reshape(rows, width), pairs[0]))
    columns = column_blocks(ids, encoder, parts)
    columns = [columns[0]] + [flip(columns[r], r) for r in range(1, parts)]
    tiles = tile_mask.shape[2]
    flags = tile_mask.reshape(1, tiles, 1).astype(jnp.bfloat16)
    flags = jnp.broadcast_to(flags, (FLAG_ROWS, tiles, block // tiles)).reshape(FLAG_ROWS, block)
    piece = jnp.concatenate(columns + [flags], axis=0)
    piece, states, ahead = lax.optimization_barrier((piece, states, ahead))
    gathered = lax.all_gather(piece, "cand", axis=0)

    pairs.append((states, to_sib(states)))
    states = to_next(states)
    if parts == 4:
        query_parts = [w_query, ahead[0], flip(lower, 1), flip(upper, 2), ahead[1]]
        query_parts += [flip(ahead[0], 2), flip(ahead[1], 1)]
    else:
        query_parts = [w_query, ahead[0]] + [flip(w_query, r) for r in range(2, parts)]
    query_parts, w_out = lax.optimization_barrier((query_parts, w_out))
    out_parts = [w_out] + [flip(w_out, r) for r in range(1, parts if parts != 4 else 3)]

    f32, bf16 = jnp.float32, jnp.bfloat16
    elen = devices * rows
    if parts == 4:
        plan = [(0, (0,), f32), (0, (2,), f32), (0, (1, 3), bf16)]
        plan += [(1, (0,), f32), (1, (1,), f32), (1, (2, 3), bf16)]
    else:
        plan = [(which, (r,), bf16 if r else f32) for which in range(2) for r in range(parts)]
    is_open, *sums = key_value(plan, gathered, w_key, w_value, parts, rows, tiles)
    sums, out_parts, states = lax.optimization_barrier((sums, out_parts, states))
    pairs.append((states, to_sib(states)))
    top = to_next(states[: clen // 2])
    if parts == 4:
        (key, key_far, key_sent), (value, value_far, value_sent) = sums[:3], sums[3:]
        came = [flip(key_sent, 1), flip(value_sent, 2)]
        came, out_parts, top = lax.optimization_barrier((came, out_parts, top))
        came = [rows_in.astype(f32) for rows_in in came]
        far = [(key_far + came[0][elen:]).astype(bf16), (value_far + came[1][elen:]).astype(bf16)]
        far = lax.optimization_barrier((flip(far[0], 2), flip(far[1], 1)))
        projected = [
            (own + near[:elen] + last.astype(f32)).astype(bf16)
            for own, near, last in zip((key, value), came, far)
        ]
    else:
        projected = []
        for own, *others in (sums[:parts], sums[parts:]):
            for r in range(1, parts):
                own = own + flip(others[r - 1], r).astype(f32)
            projected.append(own.astype(bf16))
    if parts == 4:
        out_parts += corner(*out_parts)
    out_chunks = [out_parts[: parts // 2], out_parts[parts // 2 :]]

    states = jnp.concatenate([top, to_next(states[clen // 2 :])], axis=0)
    for hop in range(3, chips):
        pairs.append((states, to_sib(states)))
        if hop < chips - 1:
            states = to_next(states)

    steps = list(range(1, chips)) + [0]
    passed = [None] * len(out_chunks)
    queries = query(ids, *pairs[steps[0]], query_parts, parts)
    for index, step in enumerate(steps):
        context = attend(order, step, ids, queries, is_open, *projected)
        sums, totals = [], []
        for chunk, weights in enumerate(out_chunks):
            if index == 1 and not chunk:
                context, passed[0] = lax.optimization_barrier((context, passed[0]))
            mine, sib = project(context, weights)
            other = to_sib(sib)
            sums.append((mine, other))
            total = mine.astype(f32) + other.astype(f32)
            if index:
                total = total + passed[chunk].astype(f32)
            totals.append(total.astype(bf16))
            if not index and not chunk:
                context, totals[0] = lax.optimization_barrier((context, totals[0]))
        if step:
            passed = [to_next(total) for total in totals]
            queries = query(ids, *pairs[steps[index + 1]], query_parts, parts)
    last = [part for (mine, other), came in zip(sums, passed) for part in (mine, other, came)]
    return finish(ids, counts, last, parts, width).reshape(cand_states.shape)


def solution(mesh):
    parts, devices = mesh.shape["prod"], mesh.shape["cand"]
    return jax.shard_map(
        functools.partial(shards, parts, devices),
        mesh=mesh,
        in_specs=(
            P("prod", "cand", None, None),
            P("prod", "cand", None),
            P("prod", "cand"),
            P("prod", "cand"),
            P("prod", "cand"),
            P("cand", "prod"),
            P("prod", "cand", None),
            P("prod"),
        ),
        out_specs=P("prod", "cand", None, None),
        check_vma=False,
    )
```

```python
import functools

import jax
import jax.numpy as jnp
from jax import lax
from jax.experimental import pallas as pl
from jax.experimental.pallas import tpu as pltpu
from jax.sharding import PartitionSpec as P

HD = 64
TILE = 128
LANES = 128
FLAG_ROWS = 16
VMEM = pltpu.CompilerParams(vmem_limit_bytes=40 * 1024 * 1024)


def ring_order(chips):
    odd = list(range(1, chips, 2))
    even = list(range(2, chips, 2))
    return [0] + odd + even[::-1]


def small():
    return pl.CostEstimate(flops=1, bytes_accessed=1, transcendentals=0)


def columns_kernel(ids, x_ref, *outs):
    block = outs[0].shape[1]
    for r, out in enumerate(outs):
        source = jnp.bitwise_xor(ids[0], r)
        out[...] = x_ref[:, pl.ds(pl.multiple_of(source * block, block), block)]


def column_blocks(ids, x, parts):
    shape = jax.ShapeDtypeStruct((x.shape[0], x.shape[1] // parts), x.dtype)
    return pl.pallas_call(
        columns_kernel,
        out_shape=[shape] * parts,
        in_specs=[
            pl.BlockSpec(memory_space=pltpu.SMEM),
            pl.BlockSpec(memory_space=pltpu.VMEM),
        ],
        out_specs=[pl.BlockSpec(memory_space=pltpu.VMEM)] * parts,
        compiler_params=VMEM,
        cost_estimate=small(),
        name="columns",
    )(ids, x)


def key_value_kernel(parts, rows, tiles, tile_of, enc_ref, w_key, w_value, open_ref, *outs):
    slots, height, block = enc_ref.shape
    local = w_key.shape[1]
    encoder = jnp.concatenate([enc_ref[slot, : parts * rows, :] for slot in range(slots)], axis=0)
    for column, weight in ((0, w_key), (local, w_value)):
        sums = jnp.dot(encoder, weight[...], preferred_element_type=jnp.float32)
        for slot in range(slots):
            for r in range(parts):
                start = (slot * parts + r) * rows
                outs[r][slot * rows : (slot + 1) * rows, column : column + local] = sums[
                    start : start + rows
                ].astype(outs[r].dtype)
    elen = slots * rows
    tile = lax.broadcasted_iota(jnp.int32, (1, elen), 1) // tile_of
    for slot in range(slots):
        seen = jnp.zeros((1, elen), jnp.float32)
        for t in range(tiles):
            start = t * (block // tiles)
            flag = enc_ref[slot, height - 1 : height, start : start + elen].astype(jnp.float32)
            seen = jnp.where(tile == t, flag, seen)
        open_ref[slot : slot + 1, :] = seen


def key_value(gathered, w_key, w_value, parts, rows, tiles):
    slots, local = gathered.shape[0], w_key.shape[1]
    elen = slots * rows
    return pl.pallas_call(
        functools.partial(key_value_kernel, parts, rows, tiles, TILE),
        out_shape=[jax.ShapeDtypeStruct((slots, elen), jnp.float32)]
        + [
            jax.ShapeDtypeStruct((elen, 2 * local), jnp.float32 if r == 0 else jnp.bfloat16)
            for r in range(parts)
        ],
        in_specs=[pl.BlockSpec(memory_space=pltpu.VMEM)] * 3,
        out_specs=[pl.BlockSpec(memory_space=pltpu.VMEM)] * (parts + 1),
        compiler_params=pltpu.CompilerParams(vmem_limit_bytes=58 * 1024 * 1024),
        cost_estimate=small(),
        name="key_value",
    )(gathered, w_key, w_value)


def query_kernel(pieces, parts, ids, mine, sib, *refs):
    weights, out_ref = refs[:pieces], refs[pieces]
    clen, width = mine.shape
    block = width // parts
    scales = []
    for ref in (mine, sib):
        values = ref[...].astype(jnp.float32)
        scales.append(lax.rsqrt(jnp.sum(values * values, axis=-1, keepdims=True) / width + 1e-06))
    total, start = None, 0
    for weight in weights:
        depth = weight.shape[0]
        from_prod = jnp.bitwise_xor(ids[0], start // block)
        source = pl.multiple_of(from_prod * block + start % block, LANES)
        rows = jnp.concatenate(
            [
                (ref[:, pl.ds(source, depth)].astype(jnp.float32) * scale).astype(jnp.bfloat16)
                for ref, scale in zip((mine, sib), scales)
            ],
            axis=0,
        )
        term = jnp.dot(rows, weight[...], preferred_element_type=jnp.float32)
        total = term if total is None else total + term
        start += depth
    out_ref[...] = total.astype(jnp.bfloat16)


def query(ids, mine, sib, weights, parts):
    clen = mine.shape[0]
    return pl.pallas_call(
        functools.partial(query_kernel, len(weights), parts),
        out_shape=jax.ShapeDtypeStruct((2 * clen, weights[0].shape[1]), jnp.bfloat16),
        in_specs=[pl.BlockSpec(memory_space=pltpu.SMEM)]
        + [pl.BlockSpec(memory_space=pltpu.VMEM)] * (2 + len(weights)),
        out_specs=pl.BlockSpec(memory_space=pltpu.VMEM),
        compiler_params=VMEM,
        cost_estimate=small(),
        name="query",
    )(ids, mine, sib, *weights)


def attend_kernel(order, step, ids, query_ref, open_ref, kv_ref, out_ref):
    chips = len(order)
    chip, core = lax.div(ids[1], 2), lax.rem(ids[1], 2)
    source = chip
    if step:
        for place in range(chips):
            source = jnp.where(chip == order[place], order[(place - step) % chips], source)
    who = (2 * source + core, 2 * source + 1 - core)
    clen = query_ref.shape[0] // 2
    elen, local = kv_ref.shape[0], kv_ref.shape[1] // 2
    is_open = (
        jnp.concatenate(
            [jnp.broadcast_to(open_ref[pl.ds(who[i], 1), :], (clen, elen)) for i in range(2)],
            axis=0,
        )
        > 0.5
    )
    lane = lax.broadcasted_iota(jnp.int32, (elen, LANES), 1) // HD
    for pair in range(local // LANES):
        columns = slice(pair * LANES, (pair + 1) * LANES)
        keys = kv_ref[:, columns]
        values = kv_ref[:, local + pair * LANES : local + (pair + 1) * LANES]
        context = None
        for half in range(LANES // HD):
            own = lane == half
            scores = (
                lax.dot_general(
                    query_ref[:, columns],
                    jnp.where(own, keys, jnp.zeros_like(keys)),
                    (((1,), (1,)), ((), ())),
                    preferred_element_type=jnp.float32,
                )
                * 0.125
            )
            scores = jnp.where(is_open, scores, -1e30)
            top = jnp.max(scores, axis=-1, keepdims=True)
            grown = jnp.exp(scores - top)
            probs = (grown / jnp.sum(grown, axis=-1, keepdims=True)).astype(jnp.bfloat16)
            term = jnp.dot(
                probs,
                jnp.where(own, values, jnp.zeros_like(values)),
                preferred_element_type=jnp.float32,
            )
            context = term if context is None else context + term
        out_ref[:, columns] = context.astype(jnp.bfloat16)


def attend(order, step, ids, queries, is_open, kv):
    return pl.pallas_call(
        functools.partial(attend_kernel, order, step),
        out_shape=jax.ShapeDtypeStruct(queries.shape, jnp.bfloat16),
        in_specs=[pl.BlockSpec(memory_space=pltpu.SMEM)]
        + [pl.BlockSpec(memory_space=pltpu.VMEM)] * 3,
        out_specs=pl.BlockSpec(memory_space=pltpu.VMEM),
        compiler_params=VMEM,
        cost_estimate=small(),
        name="attend",
    )(ids, queries, is_open, kv)


def project_kernel(pieces, context_ref, *refs):
    weights, (mine, sib) = refs[: len(pieces)], refs[len(pieces) :]
    clen = mine.shape[0]
    totals = {}
    for (r, row), weight in zip(pieces, weights):
        term = jnp.dot(
            context_ref[:, row : row + weight.shape[0]],
            weight[...],
            preferred_element_type=jnp.float32,
        )
        totals[r] = term if r not in totals else totals[r] + term
        if row + weight.shape[0] == context_ref.shape[1]:
            block = weight.shape[1]
            rows = totals[r].astype(jnp.bfloat16)
            mine[:, r * block : (r + 1) * block] = rows[:clen]
            sib[:, r * block : (r + 1) * block] = rows[clen:]


def project(context, weights):
    rows, local = context.shape
    pieces, row = [], 0
    for weight in weights:
        pieces.append((row // local, row % local))
        row += weight.shape[0]
    width = row // local * weights[0].shape[1]
    shape = jax.ShapeDtypeStruct((rows // 2, width), jnp.bfloat16)
    return pl.pallas_call(
        functools.partial(project_kernel, pieces),
        out_shape=[shape, shape],
        in_specs=[pl.BlockSpec(memory_space=pltpu.VMEM)] * (1 + len(weights)),
        out_specs=[pl.BlockSpec(memory_space=pltpu.VMEM)] * 2,
        compiler_params=VMEM,
        cost_estimate=small(),
        name="project",
    )(context, *weights)


def finish_kernel(parts, ids, counts, *refs):
    out_ref = refs[-1]
    chunks = (len(refs) - 1) // 3
    block = out_ref.shape[1] // parts
    live = jnp.where(ids[1] < counts[0], 1.0, 0.0)
    r = 0
    for chunk in range(chunks):
        mine, other, passed = refs[3 * chunk : 3 * chunk + 3]
        for start in range(0, mine.shape[1], block):
            columns = slice(start, start + block)
            total = mine[:, columns].astype(jnp.float32) + other[:, columns].astype(jnp.float32)
            total = total + passed[:, columns].astype(jnp.float32)
            target = pl.multiple_of(jnp.bitwise_xor(ids[0], r) * block, block)
            out_ref[:, pl.ds(target, block)] = (total * live).astype(jnp.bfloat16)
            r += 1


def finish(ids, counts, sums, parts, width):
    return pl.pallas_call(
        functools.partial(finish_kernel, parts),
        out_shape=jax.ShapeDtypeStruct((sums[0].shape[0], width), jnp.bfloat16),
        in_specs=[pl.BlockSpec(memory_space=pltpu.SMEM)] * 2
        + [pl.BlockSpec(memory_space=pltpu.VMEM)] * len(sums),
        out_specs=pl.BlockSpec(memory_space=pltpu.VMEM),
        compiler_params=VMEM,
        cost_estimate=small(),
        name="finish",
    )(ids, counts, *sums)


def shards(parts, devices, cand_states, enc_rows, w_query, w_key, w_value, w_out, tile_mask, counts):
    chips = devices // 2
    order = ring_order(chips)
    along = [
        (2 * order[i] + core, 2 * order[(i + 1) % chips] + core)
        for i in range(chips)
        for core in range(2)
    ]
    across = [(c, c ^ 1) for c in range(devices)]

    def to_next(value):
        return lax.ppermute(value, "cand", along)

    def to_sib(value):
        return lax.ppermute(value, "cand", across)

    def flip(value, r):
        return lax.ppermute(value, "prod", [(q, q ^ r) for q in range(parts)])

    ids = jnp.stack([lax.axis_index("prod"), lax.axis_index("cand")]).astype(jnp.int32)

    clen, width = cand_states.shape[2:]
    states = cand_states.reshape(clen, width)
    pairs = [(states, to_sib(states))]
    top = to_next(states[: clen // 2])

    half = w_query.shape[0] // 2
    if parts == 4:
        upper, lower = w_query[:half], w_query[half:]
        first = [flip(upper, 1), flip(lower, 2)]
    else:
        first = [flip(w_query, 1)]

    rows = enc_rows.shape[1]
    block = width // parts
    columns = column_blocks(ids, enc_rows.reshape(rows, width), parts)
    columns = [columns[0]] + [flip(columns[r], r) for r in range(1, parts)]
    tiles = tile_mask.shape[2]
    flags = tile_mask.reshape(1, tiles, 1).astype(jnp.bfloat16)
    flags = jnp.broadcast_to(flags, (FLAG_ROWS, tiles, block // tiles)).reshape(FLAG_ROWS, block)
    piece = jnp.concatenate(columns + [flags], axis=0)
    piece, top, first = lax.optimization_barrier((piece, top, first))
    gathered = lax.all_gather(piece, "cand", axis=0)

    states = jnp.concatenate([top, to_next(states[clen // 2 :])], axis=0)
    pairs.append((states, to_sib(states)))
    for _ in range(2, chips):
        states = to_next(states)
        pairs.append((states, to_sib(states)))
    if parts == 4:
        corner = [flip(first[0], 2), flip(first[1], 1)]
        query_parts = [w_query, first[0], flip(lower, 1), flip(upper, 2), first[1]] + corner
    else:
        query_parts = [w_query, first[0]] + [flip(w_query, r) for r in range(2, parts)]

    query_parts, w_out = lax.optimization_barrier((query_parts, w_out))
    out_parts = [w_out] + [flip(w_out, r) for r in range(1, parts if parts != 4 else 3)]
    if parts == 4:
        half = w_out.shape[0] // 2
        out_parts += [flip(out_parts[1][:half], 2), flip(out_parts[2][half:], 1)]
    out_chunks = [out_parts[: parts // 2], out_parts[parts // 2 :]]

    is_open, *sums = key_value(gathered, w_key, w_value, parts, rows, tiles)
    kv = sums[0]
    for r in range(1, parts):
        kv = kv + flip(sums[r], r).astype(jnp.float32)
    kv = kv.astype(jnp.bfloat16)

    steps = list(range(1, chips)) + [0]
    passed = [None] * len(out_chunks)
    for index, step in enumerate(steps):
        queries = query(ids, *pairs[step], query_parts, parts)
        context = attend(order, step, ids, queries, is_open, kv)
        last, totals = [], []
        for chunk, weights in enumerate(out_chunks):
            if index == 1 and not chunk:
                context, passed[0] = lax.optimization_barrier((context, passed[0]))
            mine, sib = project(context, weights)
            other = to_sib(sib)
            last += [mine, other, passed[chunk]]
            total = mine.astype(jnp.float32) + other.astype(jnp.float32)
            if index:
                total = total + passed[chunk].astype(jnp.float32)
            totals.append(total.astype(jnp.bfloat16))
            if not index and not chunk:
                context, totals[0] = lax.optimization_barrier((context, totals[0]))
        if step:
            passed = [to_next(total) for total in totals]
    return finish(ids, counts, last, parts, width).reshape(cand_states.shape)


def solution(mesh):
    parts, devices = mesh.shape["prod"], mesh.shape["cand"]
    return jax.shard_map(
        functools.partial(shards, parts, devices),
        mesh=mesh,
        in_specs=(
            P("prod", "cand", None, None),
            P("prod", "cand", None),
            P("prod", "cand"),
            P("prod", "cand"),
            P("prod", "cand"),
            P("cand", "prod"),
            P("prod", "cand", None),
            P("prod"),
        ),
        out_specs=P("prod", "cand", None, None),
        check_vma=False,
    )
```

```python
import functools

import jax
import jax.numpy as jnp
from jax import lax
from jax.experimental import pallas as pl
from jax.experimental.pallas import tpu as pltpu
from jax.sharding import PartitionSpec as P

HD = 64
TILE = 128
LANES = 128
FLAG_ROWS = 16
VMEM = pltpu.CompilerParams(vmem_limit_bytes=40 * 1024 * 1024)


def ring_order(chips):
    odd = list(range(1, chips, 2))
    even = list(range(2, chips, 2))
    return [0] + odd + even[::-1]


def small(flops=1):
    return pl.CostEstimate(flops=flops, bytes_accessed=1, transcendentals=0)


def columns_kernel(ids, x_ref, *outs):
    block = outs[0].shape[1]
    for r, out in enumerate(outs):
        source = jnp.bitwise_xor(ids[0], r)
        out[...] = x_ref[:, pl.ds(pl.multiple_of(source * block, block), block)]


def column_blocks(ids, x, parts):
    shape = jax.ShapeDtypeStruct((x.shape[0], x.shape[1] // parts), x.dtype)
    return pl.pallas_call(
        columns_kernel,
        out_shape=[shape] * parts,
        in_specs=[
            pl.BlockSpec(memory_space=pltpu.SMEM),
            pl.BlockSpec(memory_space=pltpu.VMEM),
        ],
        out_specs=[pl.BlockSpec(memory_space=pltpu.VMEM)] * parts,
        compiler_params=VMEM,
        cost_estimate=small(),
        name="columns",
    )(ids, x)


def key_value_kernel(plan, parts, rows, tiles, enc_ref, w_key, w_value, open_ref, *outs):
    slots, height, block = enc_ref.shape
    elen = slots * rows
    encoder = jnp.concatenate([enc_ref[slot, : parts * rows, :] for slot in range(slots)], axis=0)
    for which, weight in enumerate((w_key, w_value)):
        sums = jnp.dot(encoder, weight[...], preferred_element_type=jnp.float32)
        for (kind, places, _), out in zip(plan, outs):
            if kind != which:
                continue
            for index, r in enumerate(places):
                for slot in range(slots):
                    start, target = (slot * parts + r) * rows, index * elen + slot * rows
                    out[target : target + rows, :] = sums[start : start + rows].astype(out.dtype)
    tile = lax.broadcasted_iota(jnp.int32, (1, elen), 1) // TILE
    for slot in range(slots):
        seen = jnp.zeros((1, elen), jnp.float32)
        for t in range(tiles):
            start = t * (block // tiles)
            flag = enc_ref[slot, height - 1 : height, start : start + elen].astype(jnp.float32)
            seen = jnp.where(tile == t, flag, seen)
        open_ref[slot : slot + 1, :] = seen


def key_value(plan, gathered, w_key, w_value, parts, rows, tiles):
    slots, local = gathered.shape[0], w_key.shape[1]
    elen = slots * rows
    return pl.pallas_call(
        functools.partial(key_value_kernel, plan, parts, rows, tiles),
        out_shape=[jax.ShapeDtypeStruct((slots, elen), jnp.float32)]
        + [jax.ShapeDtypeStruct((len(places) * elen, local), kept) for _, places, kept in plan],
        in_specs=[pl.BlockSpec(memory_space=pltpu.VMEM)] * 3,
        out_specs=[pl.BlockSpec(memory_space=pltpu.VMEM)] * (len(plan) + 1),
        compiler_params=pltpu.CompilerParams(vmem_limit_bytes=58 * 1024 * 1024),
        cost_estimate=small(3 * 10**9),
        name="key_value",
    )(gathered, w_key, w_value)


def query_kernel(pieces, parts, ids, mine, sib, *refs):
    weights, out_ref = refs[:pieces], refs[pieces]
    clen, width = mine.shape
    block = width // parts
    scales = []
    for ref in (mine, sib):
        values = ref[...].astype(jnp.float32)
        scales.append(lax.rsqrt(jnp.sum(values * values, axis=-1, keepdims=True) / width + 1e-06))
    total, start = None, 0
    for weight in weights:
        depth = weight.shape[0]
        from_prod = jnp.bitwise_xor(ids[0], start // block)
        source = pl.multiple_of(from_prod * block + start % block, LANES)
        rows = jnp.concatenate(
            [
                (ref[:, pl.ds(source, depth)].astype(jnp.float32) * scale).astype(jnp.bfloat16)
                for ref, scale in zip((mine, sib), scales)
            ],
            axis=0,
        )
        term = jnp.dot(rows, weight[...], preferred_element_type=jnp.float32)
        total = term if total is None else total + term
        start += depth
    out_ref[...] = total.astype(jnp.bfloat16)


def query(ids, mine, sib, weights, parts):
    clen = mine.shape[0]
    return pl.pallas_call(
        functools.partial(query_kernel, len(weights), parts),
        out_shape=jax.ShapeDtypeStruct((2 * clen, weights[0].shape[1]), jnp.bfloat16),
        in_specs=[pl.BlockSpec(memory_space=pltpu.SMEM)]
        + [pl.BlockSpec(memory_space=pltpu.VMEM)] * (2 + len(weights)),
        out_specs=pl.BlockSpec(memory_space=pltpu.VMEM),
        compiler_params=VMEM,
        cost_estimate=small(),
        name="query",
    )(ids, mine, sib, *weights)


def attend_kernel(order, step, ids, query_ref, open_ref, key_ref, value_ref, out_ref):
    chips = len(order)
    chip, core = lax.div(ids[1], 2), lax.rem(ids[1], 2)
    source = chip
    if step:
        for place in range(chips):
            source = jnp.where(chip == order[place], order[(place - step) % chips], source)
    who = (2 * source + core, 2 * source + 1 - core)
    clen = query_ref.shape[0] // 2
    elen, local = key_ref.shape
    is_open = (
        jnp.concatenate(
            [jnp.broadcast_to(open_ref[pl.ds(who[i], 1), :], (clen, elen)) for i in range(2)],
            axis=0,
        )
        > 0.5
    )
    lane = lax.broadcasted_iota(jnp.int32, (elen, LANES), 1) // HD
    for pair in range(local // LANES):
        columns = slice(pair * LANES, (pair + 1) * LANES)
        keys, values = key_ref[:, columns], value_ref[:, columns]
        context = None
        for half in range(LANES // HD):
            own = lane == half
            scores = (
                lax.dot_general(
                    query_ref[:, columns],
                    jnp.where(own, keys, jnp.zeros_like(keys)),
                    (((1,), (1,)), ((), ())),
                    preferred_element_type=jnp.float32,
                )
                * 0.125
            )
            scores = jnp.where(is_open, scores, -1e30)
            top = jnp.max(scores, axis=-1, keepdims=True)
            grown = jnp.exp(scores - top)
            probs = (grown / jnp.sum(grown, axis=-1, keepdims=True)).astype(jnp.bfloat16)
            term = jnp.dot(
                probs,
                jnp.where(own, values, jnp.zeros_like(values)),
                preferred_element_type=jnp.float32,
            )
            context = term if context is None else context + term
        out_ref[:, columns] = context.astype(jnp.bfloat16)


def attend(order, step, ids, queries, is_open, keys, values):
    return pl.pallas_call(
        functools.partial(attend_kernel, order, step),
        out_shape=jax.ShapeDtypeStruct(queries.shape, jnp.bfloat16),
        in_specs=[pl.BlockSpec(memory_space=pltpu.SMEM)]
        + [pl.BlockSpec(memory_space=pltpu.VMEM)] * 4,
        out_specs=pl.BlockSpec(memory_space=pltpu.VMEM),
        compiler_params=VMEM,
        cost_estimate=small(),
        name="attend",
    )(ids, queries, is_open, keys, values)


def project_kernel(pieces, context_ref, *refs):
    weights, (mine, sib) = refs[: len(pieces)], refs[len(pieces) :]
    clen = mine.shape[0]
    totals = {}
    for (r, row), weight in zip(pieces, weights):
        term = jnp.dot(
            context_ref[:, row : row + weight.shape[0]],
            weight[...],
            preferred_element_type=jnp.float32,
        )
        totals[r] = term if r not in totals else totals[r] + term
        if row + weight.shape[0] == context_ref.shape[1]:
            block = weight.shape[1]
            rows = totals[r].astype(jnp.bfloat16)
            mine[:, r * block : (r + 1) * block] = rows[:clen]
            sib[:, r * block : (r + 1) * block] = rows[clen:]


def project(context, weights):
    rows, local = context.shape
    pieces, row = [], 0
    for weight in weights:
        pieces.append((row // local, row % local))
        row += weight.shape[0]
    width = row // local * weights[0].shape[1]
    shape = jax.ShapeDtypeStruct((rows // 2, width), jnp.bfloat16)
    return pl.pallas_call(
        functools.partial(project_kernel, pieces),
        out_shape=[shape, shape],
        in_specs=[pl.BlockSpec(memory_space=pltpu.VMEM)] * (1 + len(weights)),
        out_specs=[pl.BlockSpec(memory_space=pltpu.VMEM)] * 2,
        compiler_params=VMEM,
        cost_estimate=small(),
        name="project",
    )(context, *weights)


def finish_kernel(parts, ids, counts, *refs):
    out_ref = refs[-1]
    chunks = (len(refs) - 1) // 3
    block = out_ref.shape[1] // parts
    live = jnp.where(ids[1] < counts[0], 1.0, 0.0)
    r = 0
    for chunk in range(chunks):
        mine, other, passed = refs[3 * chunk : 3 * chunk + 3]
        for start in range(0, mine.shape[1], block):
            columns = slice(start, start + block)
            total = mine[:, columns].astype(jnp.float32) + other[:, columns].astype(jnp.float32)
            total = total + passed[:, columns].astype(jnp.float32)
            target = pl.multiple_of(jnp.bitwise_xor(ids[0], r) * block, block)
            out_ref[:, pl.ds(target, block)] = (total * live).astype(jnp.bfloat16)
            r += 1


def finish(ids, counts, sums, parts, width):
    return pl.pallas_call(
        functools.partial(finish_kernel, parts),
        out_shape=jax.ShapeDtypeStruct((sums[0].shape[0], width), jnp.bfloat16),
        in_specs=[pl.BlockSpec(memory_space=pltpu.SMEM)] * 2
        + [pl.BlockSpec(memory_space=pltpu.VMEM)] * len(sums),
        out_specs=pl.BlockSpec(memory_space=pltpu.VMEM),
        compiler_params=VMEM,
        cost_estimate=small(),
        name="finish",
    )(ids, counts, *sums)


def shards(parts, devices, cand_states, enc_rows, w_query, w_key, w_value, w_out, tile_mask, counts):
    chips = devices // 2
    order = ring_order(chips)
    along = [
        (2 * order[i] + core, 2 * order[(i + 1) % chips] + core)
        for i in range(chips)
        for core in range(2)
    ]
    across = [(c, c ^ 1) for c in range(devices)]

    def to_next(value):
        return lax.ppermute(value, "cand", along)

    def to_sib(value):
        return lax.ppermute(value, "cand", across)

    def flip(value, r):
        return lax.ppermute(value, "prod", [(q, q ^ r) for q in range(parts)])

    ids = jnp.stack([lax.axis_index("prod"), lax.axis_index("cand")]).astype(jnp.int32)

    barrier = lax.optimization_barrier
    f32, bf16 = jnp.float32, jnp.bfloat16

    def near_blocks(weight):
        return [flip(weight, r) for r in range(1, min(parts, 3))]

    def far_blocks(weight, near):
        if parts != 4:
            return [flip(weight, r) for r in range(3, parts)]
        half = weight.shape[0] // 2
        return [flip(near[0][:half], 2), flip(near[1][half:], 1)]

    clen, width = cand_states.shape[2:]
    states = cand_states.reshape(clen, width)
    pairs = [(states, to_sib(states))]
    cut = clen // 4
    top = to_next(states[:cut])

    rows = enc_rows.shape[1]
    block = width // parts
    columns = column_blocks(ids, enc_rows.reshape(rows, width), parts)
    columns = [columns[0]] + [flip(columns[r], r) for r in range(1, parts)]
    columns, w_query = barrier((columns, w_query))
    tiles = tile_mask.shape[2]
    flags = tile_mask.reshape(1, tiles, 1).astype(bf16)
    flags = jnp.broadcast_to(flags, (FLAG_ROWS, tiles, block // tiles)).reshape(FLAG_ROWS, block)
    piece = jnp.concatenate(columns + [flags], axis=0)
    piece, top = barrier((piece, top))
    gathered = lax.all_gather(piece, "cand", axis=0)
    states = jnp.concatenate([top, to_next(states[cut:])], axis=0)
    pairs.append((states, to_sib(states)))
    for hop in range(2, chips):
        if hop < chips - 1:
            states = to_next(states)
        else:
            states = jnp.concatenate([to_next(states[:-cut]), to_next(states[-cut:])], axis=0)
        pairs.append((states, to_sib(states)))

    near = near_blocks(w_query)
    query_parts = [w_query] + near + far_blocks(w_query, near)
    near, w_out = barrier((near, w_out))
    out_near = near_blocks(w_out)

    plan = [(which, (r,), bf16 if r else f32) for which in range(2) for r in range(parts)]
    is_open, *sums = key_value(plan, gathered, w_key, w_value, parts, rows, tiles)
    sums, out_near = barrier((sums, out_near))
    out_parts = [w_out] + out_near + far_blocks(w_out, out_near)
    out_chunks = [out_parts[: parts // 2], out_parts[parts // 2 :]]
    projected = []
    for own, *others in (sums[:parts], sums[parts:]):
        for r in range(1, parts):
            own = own + flip(others[r - 1], r).astype(f32)
        projected.append(own.astype(bf16))

    steps = list(range(1, chips)) + [0]
    passed = [None] * len(out_chunks)
    for index, step in enumerate(steps):
        queries = query(ids, *pairs[step], query_parts, parts)
        context = attend(order, step, ids, queries, is_open, *projected)
        last, totals = [], []
        for chunk, weights in enumerate(out_chunks):
            if index == 1 and not chunk:
                context, passed[0] = barrier((context, passed[0]))
            mine, sib = project(context, weights)
            other = to_sib(sib)
            last += [mine, other, passed[chunk]]
            total = mine.astype(f32) + other.astype(f32)
            if index:
                total = total + passed[chunk].astype(f32)
            totals.append(total.astype(bf16))
        if step:
            passed = [to_next(total) for total in totals]
    return finish(ids, counts, last, parts, width).reshape(cand_states.shape)


def solution(mesh):
    parts, devices = mesh.shape["prod"], mesh.shape["cand"]
    return jax.shard_map(
        functools.partial(shards, parts, devices),
        mesh=mesh,
        in_specs=(
            P("prod", "cand", None, None),
            P("prod", "cand", None),
            P("prod", "cand"),
            P("prod", "cand"),
            P("prod", "cand"),
            P("cand", "prod"),
            P("prod", "cand", None),
            P("prod"),
        ),
        out_specs=P("prod", "cand", None, None),
        check_vma=False,
    )
```

```python
import functools

import jax
import jax.numpy as jnp
from jax import lax
from jax.experimental import pallas as pl
from jax.experimental.pallas import tpu as pltpu
from jax.sharding import PartitionSpec as P

HD = 64
TILE = 128
LANES = 128
FLAG_ROWS = 16
VMEM = pltpu.CompilerParams(vmem_limit_bytes=40 * 1024 * 1024)


def ring_order(chips):
    odd = list(range(1, chips, 2))
    even = list(range(2, chips, 2))
    return [0] + odd + even[::-1]


def small(flops=1):
    return pl.CostEstimate(flops=flops, bytes_accessed=1, transcendentals=0)


def columns_kernel(ids, x_ref, *outs):
    block = outs[0].shape[1]
    for r, out in enumerate(outs):
        source = jnp.bitwise_xor(ids[0], r)
        out[...] = x_ref[:, pl.ds(pl.multiple_of(source * block, block), block)]


def column_blocks(ids, x, parts):
    shape = jax.ShapeDtypeStruct((x.shape[0], x.shape[1] // parts), x.dtype)
    return pl.pallas_call(
        columns_kernel,
        out_shape=[shape] * parts,
        in_specs=[
            pl.BlockSpec(memory_space=pltpu.SMEM),
            pl.BlockSpec(memory_space=pltpu.VMEM),
        ],
        out_specs=[pl.BlockSpec(memory_space=pltpu.VMEM)] * parts,
        compiler_params=VMEM,
        cost_estimate=small(),
        name="columns",
    )(ids, x)


def key_value_kernel(parts, rows, tiles, enc_ref, w_key, w_value, open_ref, *outs):
    slots, height, block = enc_ref.shape
    local = w_key.shape[1]
    elen = slots * rows
    encoder = jnp.concatenate([enc_ref[slot, : parts * rows, :] for slot in range(slots)], axis=0)
    for column, weight in ((0, w_key), (local, w_value)):
        sums = jnp.dot(encoder, weight[...], preferred_element_type=jnp.float32)
        for r, out in enumerate(outs):
            for slot in range(slots):
                start, target = (slot * parts + r) * rows, slot * rows
                out[target : target + rows, column : column + local] = sums[
                    start : start + rows
                ].astype(out.dtype)
    tile = lax.broadcasted_iota(jnp.int32, (1, elen), 1) // TILE
    for slot in range(slots):
        seen = jnp.zeros((1, elen), jnp.float32)
        for t in range(tiles):
            start = t * (block // tiles)
            flag = enc_ref[slot, height - 1 : height, start : start + elen].astype(jnp.float32)
            seen = jnp.where(tile == t, flag, seen)
        open_ref[slot : slot + 1, :] = seen


def key_value(gathered, w_key, w_value, parts, rows, tiles):
    slots, local = gathered.shape[0], w_key.shape[1]
    elen = slots * rows
    return pl.pallas_call(
        functools.partial(key_value_kernel, parts, rows, tiles),
        out_shape=[jax.ShapeDtypeStruct((slots, elen), jnp.float32)]
        + [
            jax.ShapeDtypeStruct((elen, 2 * local), jnp.bfloat16 if r else jnp.float32)
            for r in range(parts)
        ],
        in_specs=[pl.BlockSpec(memory_space=pltpu.VMEM)] * 3,
        out_specs=[pl.BlockSpec(memory_space=pltpu.VMEM)] * (parts + 1),
        compiler_params=pltpu.CompilerParams(vmem_limit_bytes=58 * 1024 * 1024),
        cost_estimate=small(3 * 10**9),
        name="key_value",
    )(gathered, w_key, w_value)


def query_kernel(pieces, parts, ids, mine, sib, *refs):
    weights, out_ref = refs[:pieces], refs[pieces]
    clen, width = mine.shape
    block = width // parts
    scales = []
    for ref in (mine, sib):
        values = ref[...].astype(jnp.float32)
        scales.append(lax.rsqrt(jnp.sum(values * values, axis=-1, keepdims=True) / width + 1e-06))
    total, start = None, 0
    for weight in weights:
        depth = weight.shape[0]
        from_prod = jnp.bitwise_xor(ids[0], start // block)
        source = pl.multiple_of(from_prod * block + start % block, LANES)
        rows = jnp.concatenate(
            [
                (ref[:, pl.ds(source, depth)].astype(jnp.float32) * scale).astype(jnp.bfloat16)
                for ref, scale in zip((mine, sib), scales)
            ],
            axis=0,
        )
        term = jnp.dot(rows, weight[...], preferred_element_type=jnp.float32)
        total = term if total is None else total + term
        start += depth
    out_ref[...] = total.astype(jnp.bfloat16)


def query(ids, mine, sib, weights, parts):
    clen = mine.shape[0]
    return pl.pallas_call(
        functools.partial(query_kernel, len(weights), parts),
        out_shape=jax.ShapeDtypeStruct((2 * clen, weights[0].shape[1]), jnp.bfloat16),
        in_specs=[pl.BlockSpec(memory_space=pltpu.SMEM)]
        + [pl.BlockSpec(memory_space=pltpu.VMEM)] * (2 + len(weights)),
        out_specs=pl.BlockSpec(memory_space=pltpu.VMEM),
        compiler_params=VMEM,
        cost_estimate=small(),
        name="query",
    )(ids, mine, sib, *weights)


def attend_kernel(order, step, ids, query_ref, open_ref, kv_ref, out_ref):
    chips = len(order)
    chip, core = lax.div(ids[1], 2), lax.rem(ids[1], 2)
    source = chip
    if step:
        for place in range(chips):
            source = jnp.where(chip == order[place], order[(place - step) % chips], source)
    who = (2 * source + core, 2 * source + 1 - core)
    clen = query_ref.shape[0] // 2
    elen, local = kv_ref.shape[0], kv_ref.shape[1] // 2
    is_open = (
        jnp.concatenate(
            [jnp.broadcast_to(open_ref[pl.ds(who[i], 1), :], (clen, elen)) for i in range(2)],
            axis=0,
        )
        > 0.5
    )
    lane = lax.broadcasted_iota(jnp.int32, (elen, LANES), 1) // HD
    for pair in range(local // LANES):
        columns = slice(pair * LANES, (pair + 1) * LANES)
        keys = kv_ref[:, columns]
        values = kv_ref[:, local + pair * LANES : local + (pair + 1) * LANES]
        context = None
        for half in range(LANES // HD):
            own = lane == half
            scores = (
                lax.dot_general(
                    query_ref[:, columns],
                    jnp.where(own, keys, jnp.zeros_like(keys)),
                    (((1,), (1,)), ((), ())),
                    preferred_element_type=jnp.float32,
                )
                * 0.125
            )
            scores = jnp.where(is_open, scores, -1e30)
            top = jnp.max(scores, axis=-1, keepdims=True)
            grown = jnp.exp(scores - top)
            probs = (grown / jnp.sum(grown, axis=-1, keepdims=True)).astype(jnp.bfloat16)
            term = jnp.dot(
                probs,
                jnp.where(own, values, jnp.zeros_like(values)),
                preferred_element_type=jnp.float32,
            )
            context = term if context is None else context + term
        out_ref[:, columns] = context.astype(jnp.bfloat16)


def attend(order, step, ids, queries, is_open, kv):
    return pl.pallas_call(
        functools.partial(attend_kernel, order, step),
        out_shape=jax.ShapeDtypeStruct(queries.shape, jnp.bfloat16),
        in_specs=[pl.BlockSpec(memory_space=pltpu.SMEM)]
        + [pl.BlockSpec(memory_space=pltpu.VMEM)] * 3,
        out_specs=pl.BlockSpec(memory_space=pltpu.VMEM),
        compiler_params=VMEM,
        cost_estimate=small(),
        name="attend",
    )(ids, queries, is_open, kv)


def project_kernel(pieces, context_ref, *refs):
    weights, (mine, sib) = refs[: len(pieces)], refs[len(pieces) :]
    clen = mine.shape[0]
    totals = {}
    for (r, row), weight in zip(pieces, weights):
        term = jnp.dot(
            context_ref[:, row : row + weight.shape[0]],
            weight[...],
            preferred_element_type=jnp.float32,
        )
        totals[r] = term if r not in totals else totals[r] + term
        if row + weight.shape[0] == context_ref.shape[1]:
            block = weight.shape[1]
            rows = totals[r].astype(jnp.bfloat16)
            mine[:, r * block : (r + 1) * block] = rows[:clen]
            sib[:, r * block : (r + 1) * block] = rows[clen:]


def project(context, weights):
    rows, local = context.shape
    pieces, row = [], 0
    for weight in weights:
        pieces.append((row // local, row % local))
        row += weight.shape[0]
    width = row // local * weights[0].shape[1]
    shape = jax.ShapeDtypeStruct((rows // 2, width), jnp.bfloat16)
    return pl.pallas_call(
        functools.partial(project_kernel, pieces),
        out_shape=[shape, shape],
        in_specs=[pl.BlockSpec(memory_space=pltpu.VMEM)] * (1 + len(weights)),
        out_specs=[pl.BlockSpec(memory_space=pltpu.VMEM)] * 2,
        compiler_params=VMEM,
        cost_estimate=small(),
        name="project",
    )(context, *weights)


def finish_kernel(parts, ids, counts, *refs):
    out_ref = refs[-1]
    chunks = (len(refs) - 1) // 3
    block = out_ref.shape[1] // parts
    live = jnp.where(ids[1] < counts[0], 1.0, 0.0)
    r = 0
    for chunk in range(chunks):
        mine, other, passed = refs[3 * chunk : 3 * chunk + 3]
        for start in range(0, mine.shape[1], block):
            columns = slice(start, start + block)
            total = mine[:, columns].astype(jnp.float32) + other[:, columns].astype(jnp.float32)
            total = total + passed[:, columns].astype(jnp.float32)
            target = pl.multiple_of(jnp.bitwise_xor(ids[0], r) * block, block)
            out_ref[:, pl.ds(target, block)] = (total * live).astype(jnp.bfloat16)
            r += 1


def finish(ids, counts, sums, parts, width):
    return pl.pallas_call(
        functools.partial(finish_kernel, parts),
        out_shape=jax.ShapeDtypeStruct((sums[0].shape[0], width), jnp.bfloat16),
        in_specs=[pl.BlockSpec(memory_space=pltpu.SMEM)] * 2
        + [pl.BlockSpec(memory_space=pltpu.VMEM)] * len(sums),
        out_specs=pl.BlockSpec(memory_space=pltpu.VMEM),
        compiler_params=VMEM,
        cost_estimate=small(),
        name="finish",
    )(ids, counts, *sums)


def shards(parts, devices, cand_states, enc_rows, w_query, w_key, w_value, w_out, tile_mask, counts):
    chips = devices // 2
    order = ring_order(chips)
    along = [
        (2 * order[i] + core, 2 * order[(i + 1) % chips] + core)
        for i in range(chips)
        for core in range(2)
    ]
    across = [(c, c ^ 1) for c in range(devices)]

    def to_next(value):
        return lax.ppermute(value, "cand", along)

    def to_sib(value):
        return lax.ppermute(value, "cand", across)

    def flip(value, r):
        return lax.ppermute(value, "prod", [(q, q ^ r) for q in range(parts)])

    ids = jnp.stack([lax.axis_index("prod"), lax.axis_index("cand")]).astype(jnp.int32)

    barrier = lax.optimization_barrier
    f32, bf16 = jnp.float32, jnp.bfloat16

    def near_blocks(weight):
        return [flip(weight, r) for r in range(1, min(parts, 3))]

    def far_blocks(weight, near):
        if parts != 4:
            return [flip(weight, r) for r in range(3, parts)]
        half = weight.shape[0] // 2
        return [flip(near[0][:half], 2), flip(near[1][half:], 1)]

    clen, width = cand_states.shape[2:]
    states = cand_states.reshape(clen, width)
    pairs = [(states, to_sib(states))]
    cut = clen // 4
    top = to_next(states[:cut])

    rows = enc_rows.shape[1]
    block = width // parts
    columns = column_blocks(ids, enc_rows.reshape(rows, width), parts)
    columns = [columns[0]] + [flip(columns[r], r) for r in range(1, parts)]
    columns, w_query = barrier((columns, w_query))
    tiles = tile_mask.shape[2]
    flags = tile_mask.reshape(1, tiles, 1).astype(bf16)
    flags = jnp.broadcast_to(flags, (FLAG_ROWS, tiles, block // tiles)).reshape(FLAG_ROWS, block)
    piece = jnp.concatenate(columns + [flags], axis=0)
    piece, top = barrier((piece, top))
    gathered = lax.all_gather(piece, "cand", axis=0)
    states = jnp.concatenate([top, to_next(states[cut:])], axis=0)
    pairs.append((states, to_sib(states)))
    for hop in range(2, chips):
        states = to_next(states)
        pairs.append((states, to_sib(states)))

    near = near_blocks(w_query)
    query_parts = [w_query] + near + far_blocks(w_query, near)
    near, w_out = barrier((near, w_out))
    out_near = near_blocks(w_out)

    is_open, *sums = key_value(gathered, w_key, w_value, parts, rows, tiles)
    sums, out_near = barrier((sums, out_near))
    out_parts = [w_out] + out_near + far_blocks(w_out, out_near)
    out_chunks = [out_parts[: parts // 2], out_parts[parts // 2 :]]
    kv = sums[0]
    for r in range(1, parts):
        kv = kv + flip(sums[r], r).astype(f32)
    kv = kv.astype(bf16)

    steps = list(range(1, chips)) + [0]
    passed = [None] * len(out_chunks)
    queries = [query(ids, *pairs[step], query_parts, parts) for step in steps]
    for index, step in enumerate(steps):
        context = attend(order, step, ids, queries[index], is_open, kv)
        last, totals = [], []
        for chunk, weights in enumerate(out_chunks):
            if index == 1 and not chunk:
                context, passed[0] = barrier((context, passed[0]))
            mine, sib = project(context, weights)
            other = to_sib(sib)
            last += [mine, other, passed[chunk]]
            total = mine.astype(f32) + other.astype(f32)
            if index:
                total = total + passed[chunk].astype(f32)
            totals.append(total.astype(bf16))
        if not index:
            totals[1], queries[1] = barrier((totals[1], queries[1]))
        if step:
            passed = [to_next(total) for total in totals]
    return finish(ids, counts, last, parts, width).reshape(cand_states.shape)


def solution(mesh):
    parts, devices = mesh.shape["prod"], mesh.shape["cand"]
    return jax.shard_map(
        functools.partial(shards, parts, devices),
        mesh=mesh,
        in_specs=(
            P("prod", "cand", None, None),
            P("prod", "cand", None),
            P("prod", "cand"),
            P("prod", "cand"),
            P("prod", "cand"),
            P("cand", "prod"),
            P("prod", "cand", None),
            P("prod"),
        ),
        out_specs=P("prod", "cand", None, None),
        check_vma=False,
    )
```

```python
import functools

import jax
import jax.numpy as jnp
from jax import lax
from jax.experimental import pallas as pl
from jax.experimental.pallas import tpu as pltpu
from jax.sharding import PartitionSpec as P

HD = 64
TILE = 128
LANES = 128
FLAG_ROWS = 16
VMEM = pltpu.CompilerParams(vmem_limit_bytes=40 * 1024 * 1024)


def ring_order(chips):
    odd = list(range(1, chips, 2))
    even = list(range(2, chips, 2))
    return [0] + odd + even[::-1]


def small(flops=1):
    return pl.CostEstimate(flops=flops, bytes_accessed=1, transcendentals=0)


def columns_kernel(ids, x_ref, *outs):
    block = outs[0].shape[1]
    for r, out in enumerate(outs):
        source = jnp.bitwise_xor(ids[0], r)
        out[...] = x_ref[:, pl.ds(pl.multiple_of(source * block, block), block)]


def column_blocks(ids, x, parts):
    shape = jax.ShapeDtypeStruct((x.shape[0], x.shape[1] // parts), x.dtype)
    return pl.pallas_call(
        columns_kernel,
        out_shape=[shape] * parts,
        in_specs=[
            pl.BlockSpec(memory_space=pltpu.SMEM),
            pl.BlockSpec(memory_space=pltpu.VMEM),
        ],
        out_specs=[pl.BlockSpec(memory_space=pltpu.VMEM)] * parts,
        compiler_params=VMEM,
        cost_estimate=small(),
        name="columns",
    )(ids, x)


def key_value_kernel(parts, rows, tiles, enc_ref, w_key, w_value, open_ref, *outs):
    slots, height, block = enc_ref.shape
    local = w_key.shape[1]
    elen = slots * rows
    encoder = jnp.concatenate([enc_ref[slot, : parts * rows, :] for slot in range(slots)], axis=0)
    for column, weight in ((0, w_key), (local, w_value)):
        sums = jnp.dot(encoder, weight[...], preferred_element_type=jnp.float32)
        for r, out in enumerate(outs):
            for slot in range(slots):
                start, target = (slot * parts + r) * rows, slot * rows
                out[target : target + rows, column : column + local] = sums[
                    start : start + rows
                ].astype(out.dtype)
    tile = lax.broadcasted_iota(jnp.int32, (1, elen), 1) // TILE
    for slot in range(slots):
        seen = jnp.zeros((1, elen), jnp.float32)
        for t in range(tiles):
            start = t * (block // tiles)
            flag = enc_ref[slot, height - 1 : height, start : start + elen].astype(jnp.float32)
            seen = jnp.where(tile == t, flag, seen)
        open_ref[slot : slot + 1, :] = seen


def key_value(gathered, w_key, w_value, parts, rows, tiles):
    slots, local = gathered.shape[0], w_key.shape[1]
    elen = slots * rows
    return pl.pallas_call(
        functools.partial(key_value_kernel, parts, rows, tiles),
        out_shape=[jax.ShapeDtypeStruct((slots, elen), jnp.float32)]
        + [
            jax.ShapeDtypeStruct((elen, 2 * local), jnp.bfloat16 if r else jnp.float32)
            for r in range(parts)
        ],
        in_specs=[pl.BlockSpec(memory_space=pltpu.VMEM)] * 3,
        out_specs=[pl.BlockSpec(memory_space=pltpu.VMEM)] * (parts + 1),
        compiler_params=pltpu.CompilerParams(vmem_limit_bytes=58 * 1024 * 1024),
        cost_estimate=small(3 * 10**9),
        name="key_value",
    )(gathered, w_key, w_value)


def query_kernel(pieces, parts, ids, mine, sib, *refs):
    weights, out_ref = refs[:pieces], refs[pieces]
    clen, width = mine.shape
    block = width // parts
    scales = []
    for ref in (mine, sib):
        values = ref[...].astype(jnp.float32)
        scales.append(lax.rsqrt(jnp.sum(values * values, axis=-1, keepdims=True) / width + 1e-06))
    total, start = None, 0
    for weight in weights:
        depth = weight.shape[0]
        from_prod = jnp.bitwise_xor(ids[0], start // block)
        source = pl.multiple_of(from_prod * block + start % block, LANES)
        rows = jnp.concatenate(
            [
                (ref[:, pl.ds(source, depth)].astype(jnp.float32) * scale).astype(jnp.bfloat16)
                for ref, scale in zip((mine, sib), scales)
            ],
            axis=0,
        )
        term = jnp.dot(rows, weight[...], preferred_element_type=jnp.float32)
        total = term if total is None else total + term
        start += depth
    out_ref[...] = total.astype(jnp.bfloat16)


def query(ids, mine, sib, weights, parts):
    clen = mine.shape[0]
    return pl.pallas_call(
        functools.partial(query_kernel, len(weights), parts),
        out_shape=jax.ShapeDtypeStruct((2 * clen, weights[0].shape[1]), jnp.bfloat16),
        in_specs=[pl.BlockSpec(memory_space=pltpu.SMEM)]
        + [pl.BlockSpec(memory_space=pltpu.VMEM)] * (2 + len(weights)),
        out_specs=pl.BlockSpec(memory_space=pltpu.VMEM),
        compiler_params=VMEM,
        cost_estimate=small(),
        name="query",
    )(ids, mine, sib, *weights)


def attend_kernel(order, step, ids, query_ref, open_ref, kv_ref, out_ref):
    chips = len(order)
    chip, core = lax.div(ids[1], 2), lax.rem(ids[1], 2)
    source = chip
    if step:
        for place in range(chips):
            source = jnp.where(chip == order[place], order[(place - step) % chips], source)
    who = (2 * source + core, 2 * source + 1 - core)
    clen = query_ref.shape[0] // 2
    elen, local = kv_ref.shape[0], kv_ref.shape[1] // 2
    is_open = (
        jnp.concatenate(
            [jnp.broadcast_to(open_ref[pl.ds(who[i], 1), :], (clen, elen)) for i in range(2)],
            axis=0,
        )
        > 0.5
    )
    lane = lax.broadcasted_iota(jnp.int32, (elen, LANES), 1) // HD
    for pair in range(local // LANES):
        columns = slice(pair * LANES, (pair + 1) * LANES)
        keys = kv_ref[:, columns]
        values = kv_ref[:, local + pair * LANES : local + (pair + 1) * LANES]
        context = None
        for half in range(LANES // HD):
            own = lane == half
            scores = (
                lax.dot_general(
                    query_ref[:, columns],
                    jnp.where(own, keys, jnp.zeros_like(keys)),
                    (((1,), (1,)), ((), ())),
                    preferred_element_type=jnp.float32,
                )
                * 0.125
            )
            scores = jnp.where(is_open, scores, -1e30)
            top = jnp.max(scores, axis=-1, keepdims=True)
            grown = jnp.exp(scores - top)
            probs = (grown / jnp.sum(grown, axis=-1, keepdims=True)).astype(jnp.bfloat16)
            term = jnp.dot(
                probs,
                jnp.where(own, values, jnp.zeros_like(values)),
                preferred_element_type=jnp.float32,
            )
            context = term if context is None else context + term
        out_ref[:, columns] = context.astype(jnp.bfloat16)


def attend(order, step, ids, queries, is_open, kv):
    return pl.pallas_call(
        functools.partial(attend_kernel, order, step),
        out_shape=jax.ShapeDtypeStruct(queries.shape, jnp.bfloat16),
        in_specs=[pl.BlockSpec(memory_space=pltpu.SMEM)]
        + [pl.BlockSpec(memory_space=pltpu.VMEM)] * 3,
        out_specs=pl.BlockSpec(memory_space=pltpu.VMEM),
        compiler_params=VMEM,
        cost_estimate=small(),
        name="attend",
    )(ids, queries, is_open, kv)


def project_kernel(pieces, context_ref, *refs):
    weights, (mine, sib) = refs[: len(pieces)], refs[len(pieces) :]
    clen = mine.shape[0]
    totals = {}
    for (r, row), weight in zip(pieces, weights):
        term = jnp.dot(
            context_ref[:, row : row + weight.shape[0]],
            weight[...],
            preferred_element_type=jnp.float32,
        )
        totals[r] = term if r not in totals else totals[r] + term
        if row + weight.shape[0] == context_ref.shape[1]:
            block = weight.shape[1]
            rows = totals[r].astype(jnp.bfloat16)
            mine[:, r * block : (r + 1) * block] = rows[:clen]
            sib[:, r * block : (r + 1) * block] = rows[clen:]


def project(context, weights):
    rows, local = context.shape
    pieces, row = [], 0
    for weight in weights:
        pieces.append((row // local, row % local))
        row += weight.shape[0]
    width = row // local * weights[0].shape[1]
    shape = jax.ShapeDtypeStruct((rows // 2, width), jnp.bfloat16)
    return pl.pallas_call(
        functools.partial(project_kernel, pieces),
        out_shape=[shape, shape],
        in_specs=[pl.BlockSpec(memory_space=pltpu.VMEM)] * (1 + len(weights)),
        out_specs=[pl.BlockSpec(memory_space=pltpu.VMEM)] * 2,
        compiler_params=VMEM,
        cost_estimate=small(),
        name="project",
    )(context, *weights)


def finish_kernel(parts, ids, counts, *refs):
    out_ref = refs[-1]
    chunks = (len(refs) - 1) // 3
    block = out_ref.shape[1] // parts
    live = jnp.where(ids[1] < counts[0], 1.0, 0.0)
    r = 0
    for chunk in range(chunks):
        mine, other, passed = refs[3 * chunk : 3 * chunk + 3]
        for start in range(0, mine.shape[1], block):
            columns = slice(start, start + block)
            total = mine[:, columns].astype(jnp.float32) + other[:, columns].astype(jnp.float32)
            total = total + passed[:, columns].astype(jnp.float32)
            target = pl.multiple_of(jnp.bitwise_xor(ids[0], r) * block, block)
            out_ref[:, pl.ds(target, block)] = (total * live).astype(jnp.bfloat16)
            r += 1


def finish(ids, counts, sums, parts, width):
    return pl.pallas_call(
        functools.partial(finish_kernel, parts),
        out_shape=jax.ShapeDtypeStruct((sums[0].shape[0], width), jnp.bfloat16),
        in_specs=[pl.BlockSpec(memory_space=pltpu.SMEM)] * 2
        + [pl.BlockSpec(memory_space=pltpu.VMEM)] * len(sums),
        out_specs=pl.BlockSpec(memory_space=pltpu.VMEM),
        compiler_params=VMEM,
        cost_estimate=small(),
        name="finish",
    )(ids, counts, *sums)


def shards(parts, devices, cand_states, enc_rows, w_query, w_key, w_value, w_out, tile_mask, counts):
    chips = devices // 2
    order = ring_order(chips)
    along = [
        (2 * order[i] + core, 2 * order[(i + 1) % chips] + core)
        for i in range(chips)
        for core in range(2)
    ]
    across = [(c, c ^ 1) for c in range(devices)]

    def to_next(value):
        return lax.ppermute(value, "cand", along)

    def to_sib(value):
        return lax.ppermute(value, "cand", across)

    def flip(value, r):
        return lax.ppermute(value, "prod", [(q, q ^ r) for q in range(parts)])

    ids = jnp.stack([lax.axis_index("prod"), lax.axis_index("cand")]).astype(jnp.int32)

    barrier = lax.optimization_barrier
    f32, bf16 = jnp.float32, jnp.bfloat16

    def near_blocks(weight):
        return [flip(weight, r) for r in range(1, min(parts, 3))]

    def far_blocks(weight, near):
        if parts != 4:
            return [flip(weight, r) for r in range(3, parts)]
        half = weight.shape[0] // 2
        return [flip(near[0][:half], 2), flip(near[1][half:], 1)]

    clen, width = cand_states.shape[2:]
    states = cand_states.reshape(clen, width)
    pairs = [(states, to_sib(states))]
    cut = clen // 8
    top = to_next(states[:cut])

    rows = enc_rows.shape[1]
    block = width // parts
    columns = column_blocks(ids, enc_rows.reshape(rows, width), parts)
    columns = [columns[0]] + [flip(columns[r], r) for r in range(1, parts)]
    columns, w_query = barrier((columns, w_query))
    tiles = tile_mask.shape[2]
    flags = tile_mask.reshape(1, tiles, 1).astype(bf16)
    flags = jnp.broadcast_to(flags, (FLAG_ROWS, tiles, block // tiles)).reshape(FLAG_ROWS, block)
    piece = jnp.concatenate(columns + [flags], axis=0)
    piece, top = barrier((piece, top))
    gathered = lax.all_gather(piece, "cand", axis=0)
    states = jnp.concatenate([top, to_next(states[cut:])], axis=0)
    pairs.append((states, to_sib(states)))
    for hop in range(2, chips):
        states = to_next(states)
        pairs.append((states, to_sib(states)))

    near = near_blocks(w_query)
    query_parts = [w_query] + near + far_blocks(w_query, near)
    near, w_out = barrier((near, w_out))
    out_near = near_blocks(w_out)

    is_open, *sums = key_value(gathered, w_key, w_value, parts, rows, tiles)
    sums, out_near = barrier((sums, out_near))
    out_parts = [w_out] + out_near + far_blocks(w_out, out_near)
    out_chunks = [out_parts[: parts // 2], out_parts[parts // 2 :]]
    kv = sums[0]
    for r in range(1, parts):
        kv = kv + flip(sums[r], r).astype(f32)
    kv = kv.astype(bf16)

    steps = list(range(1, chips)) + [0]
    passed = [None] * len(out_chunks)
    queries = [query(ids, *pairs[step], query_parts, parts) for step in steps]
    for index, step in enumerate(steps):
        context = attend(order, step, ids, queries[index], is_open, kv)
        last, totals = [], []
        for chunk, weights in enumerate(out_chunks):
            if index == 1 and not chunk:
                context, passed[0] = barrier((context, passed[0]))
            mine, sib = project(context, weights)
            other = to_sib(sib)
            last += [mine, other, passed[chunk]]
            total = mine.astype(f32) + other.astype(f32)
            if index:
                total = total + passed[chunk].astype(f32)
            totals.append(total.astype(bf16))
        if not index:
            totals[1], queries[1] = barrier((totals[1], queries[1]))
        if step:
            passed = [to_next(total) for total in totals]
    return finish(ids, counts, last, parts, width).reshape(cand_states.shape)


def solution(mesh):
    parts, devices = mesh.shape["prod"], mesh.shape["cand"]
    return jax.shard_map(
        functools.partial(shards, parts, devices),
        mesh=mesh,
        in_specs=(
            P("prod", "cand", None, None),
            P("prod", "cand", None),
            P("prod", "cand"),
            P("prod", "cand"),
            P("prod", "cand"),
            P("cand", "prod"),
            P("prod", "cand", None),
            P("prod"),
        ),
        out_specs=P("prod", "cand", None, None),
        check_vma=False,
    )
```

```python
import functools

import jax
import jax.numpy as jnp
from jax import lax
from jax.experimental import pallas as pl
from jax.experimental.pallas import tpu as pltpu
from jax.sharding import PartitionSpec as P

HD = 64
TILE = 128
LANES = 128
FLAG_ROWS = 16
VMEM = pltpu.CompilerParams(vmem_limit_bytes=40 * 1024 * 1024)


def ring_order(chips):
    odd = list(range(1, chips, 2))
    even = list(range(2, chips, 2))
    return [0] + odd + even[::-1]


def small(flops=1):
    return pl.CostEstimate(flops=flops, bytes_accessed=1, transcendentals=0)


def columns_kernel(ids, x_ref, *outs):
    block = outs[0].shape[1]
    for r, out in enumerate(outs):
        source = jnp.bitwise_xor(ids[0], r)
        out[...] = x_ref[:, pl.ds(pl.multiple_of(source * block, block), block)]


def column_blocks(ids, x, parts):
    shape = jax.ShapeDtypeStruct((x.shape[0], x.shape[1] // parts), x.dtype)
    return pl.pallas_call(
        columns_kernel,
        out_shape=[shape] * parts,
        in_specs=[
            pl.BlockSpec(memory_space=pltpu.SMEM),
            pl.BlockSpec(memory_space=pltpu.VMEM),
        ],
        out_specs=[pl.BlockSpec(memory_space=pltpu.VMEM)] * parts,
        compiler_params=VMEM,
        cost_estimate=small(),
        name="columns",
    )(ids, x)


def key_value_kernel(parts, rows, tiles, enc_ref, w_key, w_value, open_ref, *outs):
    slots, height, block = enc_ref.shape
    local = w_key.shape[1]
    elen = slots * rows
    encoder = jnp.concatenate([enc_ref[slot, : parts * rows, :] for slot in range(slots)], axis=0)
    for column, weight in ((0, w_key), (local, w_value)):
        sums = jnp.dot(encoder, weight[...], preferred_element_type=jnp.float32)
        for r, out in enumerate(outs):
            for slot in range(slots):
                start, target = (slot * parts + r) * rows, slot * rows
                out[target : target + rows, column : column + local] = sums[
                    start : start + rows
                ].astype(out.dtype)
    tile = lax.broadcasted_iota(jnp.int32, (1, elen), 1) // TILE
    for slot in range(slots):
        seen = jnp.zeros((1, elen), jnp.float32)
        for t in range(tiles):
            start = t * (block // tiles)
            flag = enc_ref[slot, height - 1 : height, start : start + elen].astype(jnp.float32)
            seen = jnp.where(tile == t, flag, seen)
        open_ref[slot : slot + 1, :] = seen


def key_value(gathered, w_key, w_value, parts, rows, tiles):
    slots, local = gathered.shape[0], w_key.shape[1]
    elen = slots * rows
    return pl.pallas_call(
        functools.partial(key_value_kernel, parts, rows, tiles),
        out_shape=[jax.ShapeDtypeStruct((slots, elen), jnp.float32)]
        + [
            jax.ShapeDtypeStruct((elen, 2 * local), jnp.bfloat16 if r else jnp.float32)
            for r in range(parts)
        ],
        in_specs=[pl.BlockSpec(memory_space=pltpu.VMEM)] * 3,
        out_specs=[pl.BlockSpec(memory_space=pltpu.VMEM)] * (parts + 1),
        compiler_params=pltpu.CompilerParams(vmem_limit_bytes=58 * 1024 * 1024),
        cost_estimate=small(3 * 10**9),
        name="key_value",
    )(gathered, w_key, w_value)


def query_kernel(pieces, parts, ids, mine, sib, *refs):
    weights, out_ref = refs[:pieces], refs[pieces]
    clen, width = mine.shape
    block = width // parts
    scales = []
    for ref in (mine, sib):
        values = ref[...].astype(jnp.float32)
        scales.append(lax.rsqrt(jnp.sum(values * values, axis=-1, keepdims=True) / width + 1e-06))
    total, start = None, 0
    for weight in weights:
        depth = weight.shape[0]
        from_prod = jnp.bitwise_xor(ids[0], start // block)
        source = pl.multiple_of(from_prod * block + start % block, LANES)
        rows = jnp.concatenate(
            [
                (ref[:, pl.ds(source, depth)].astype(jnp.float32) * scale).astype(jnp.bfloat16)
                for ref, scale in zip((mine, sib), scales)
            ],
            axis=0,
        )
        term = jnp.dot(rows, weight[...], preferred_element_type=jnp.float32)
        total = term if total is None else total + term
        start += depth
    out_ref[...] = total.astype(jnp.bfloat16)


def query(ids, mine, sib, weights, parts):
    clen = mine.shape[0]
    return pl.pallas_call(
        functools.partial(query_kernel, len(weights), parts),
        out_shape=jax.ShapeDtypeStruct((2 * clen, weights[0].shape[1]), jnp.bfloat16),
        in_specs=[pl.BlockSpec(memory_space=pltpu.SMEM)]
        + [pl.BlockSpec(memory_space=pltpu.VMEM)] * (2 + len(weights)),
        out_specs=pl.BlockSpec(memory_space=pltpu.VMEM),
        compiler_params=VMEM,
        cost_estimate=small(),
        name="query",
    )(ids, mine, sib, *weights)


def attend_kernel(order, step, ids, query_ref, open_ref, kv_ref, out_ref):
    chips = len(order)
    chip, core = lax.div(ids[1], 2), lax.rem(ids[1], 2)
    source = chip
    if step:
        for place in range(chips):
            source = jnp.where(chip == order[place], order[(place - step) % chips], source)
    who = (2 * source + core, 2 * source + 1 - core)
    clen = query_ref.shape[0] // 2
    elen, local = kv_ref.shape[0], kv_ref.shape[1] // 2
    is_open = (
        jnp.concatenate(
            [jnp.broadcast_to(open_ref[pl.ds(who[i], 1), :], (clen, elen)) for i in range(2)],
            axis=0,
        )
        > 0.5
    )
    lane = lax.broadcasted_iota(jnp.int32, (elen, LANES), 1) // HD
    for pair in range(local // LANES):
        columns = slice(pair * LANES, (pair + 1) * LANES)
        keys = kv_ref[:, columns]
        values = kv_ref[:, local + pair * LANES : local + (pair + 1) * LANES]
        context = None
        for half in range(LANES // HD):
            own = lane == half
            scores = (
                lax.dot_general(
                    query_ref[:, columns],
                    jnp.where(own, keys, jnp.zeros_like(keys)),
                    (((1,), (1,)), ((), ())),
                    preferred_element_type=jnp.float32,
                )
                * 0.125
            )
            scores = jnp.where(is_open, scores, -1e30)
            top = jnp.max(scores, axis=-1, keepdims=True)
            grown = jnp.exp(scores - top)
            probs = (grown / jnp.sum(grown, axis=-1, keepdims=True)).astype(jnp.bfloat16)
            term = jnp.dot(
                probs,
                jnp.where(own, values, jnp.zeros_like(values)),
                preferred_element_type=jnp.float32,
            )
            context = term if context is None else context + term
        out_ref[:, columns] = context.astype(jnp.bfloat16)


def attend(order, step, ids, queries, is_open, kv):
    return pl.pallas_call(
        functools.partial(attend_kernel, order, step),
        out_shape=jax.ShapeDtypeStruct(queries.shape, jnp.bfloat16),
        in_specs=[pl.BlockSpec(memory_space=pltpu.SMEM)]
        + [pl.BlockSpec(memory_space=pltpu.VMEM)] * 3,
        out_specs=pl.BlockSpec(memory_space=pltpu.VMEM),
        compiler_params=VMEM,
        cost_estimate=small(),
        name="attend",
    )(ids, queries, is_open, kv)


def project_kernel(count, context_ref, *refs):
    weights, (mine, sib) = refs[:count], refs[count:]
    clen = mine.shape[0]
    start = 0
    for weight in weights:
        columns = slice(start, start + weight.shape[1])
        rows = jnp.dot(context_ref[...], weight[...], preferred_element_type=jnp.float32)
        rows = rows.astype(jnp.bfloat16)
        mine[:, columns] = rows[:clen]
        sib[:, columns] = rows[clen:]
        start += weight.shape[1]


def project(context, weights):
    rows = context.shape[0]
    width = sum(weight.shape[1] for weight in weights)
    shape = jax.ShapeDtypeStruct((rows // 2, width), jnp.bfloat16)
    return pl.pallas_call(
        functools.partial(project_kernel, len(weights)),
        out_shape=[shape, shape],
        in_specs=[pl.BlockSpec(memory_space=pltpu.VMEM)] * (1 + len(weights)),
        out_specs=[pl.BlockSpec(memory_space=pltpu.VMEM)] * 2,
        compiler_params=VMEM,
        cost_estimate=small(),
        name="project",
    )(context, *weights)


def finish_kernel(parts, places, ids, counts, *refs):
    out_ref = refs[-1]
    block = out_ref.shape[1] // parts
    live = jnp.where(ids[1] < counts[0], 1.0, 0.0)
    for chunk, pieces in enumerate(places):
        mine, other, passed = refs[3 * chunk : 3 * chunk + 3]
        start = 0
        for r, offset, size in pieces:
            columns = slice(start, start + size)
            total = mine[:, columns].astype(jnp.float32) + other[:, columns].astype(jnp.float32)
            total = total + passed[:, columns].astype(jnp.float32)
            target = pl.multiple_of(jnp.bitwise_xor(ids[0], r) * block + offset, LANES)
            out_ref[:, pl.ds(target, size)] = (total * live).astype(jnp.bfloat16)
            start += size


def finish(places, ids, counts, sums, parts, width):
    return pl.pallas_call(
        functools.partial(finish_kernel, parts, places),
        out_shape=jax.ShapeDtypeStruct((sums[0].shape[0], width), jnp.bfloat16),
        in_specs=[pl.BlockSpec(memory_space=pltpu.SMEM)] * 2
        + [pl.BlockSpec(memory_space=pltpu.VMEM)] * len(sums),
        out_specs=pl.BlockSpec(memory_space=pltpu.VMEM),
        compiler_params=VMEM,
        cost_estimate=small(),
        name="finish",
    )(ids, counts, *sums)


def shards(parts, devices, cand_states, enc_rows, w_query, w_key, w_value, w_out, tile_mask, counts):
    chips = devices // 2
    order = ring_order(chips)
    along = [
        (2 * order[i] + core, 2 * order[(i + 1) % chips] + core)
        for i in range(chips)
        for core in range(2)
    ]
    across = [(c, c ^ 1) for c in range(devices)]

    def to_next(value):
        return lax.ppermute(value, "cand", along)

    def to_sib(value):
        return lax.ppermute(value, "cand", across)

    def flip(value, r):
        return lax.ppermute(value, "prod", [(q, q ^ r) for q in range(parts)])

    ids = jnp.stack([lax.axis_index("prod"), lax.axis_index("cand")]).astype(jnp.int32)

    barrier = lax.optimization_barrier
    f32, bf16 = jnp.float32, jnp.bfloat16

    def near_blocks(weight):
        return [flip(weight, r) for r in range(1, min(parts, 3))]

    def far_blocks(weight, near):
        if parts != 4:
            return [flip(weight, r) for r in range(3, parts)]
        half = weight.shape[0] // 2
        return [flip(near[0][:half], 2), flip(near[1][half:], 1)]

    clen, width = cand_states.shape[2:]
    states = cand_states.reshape(clen, width)
    pairs = [(states, to_sib(states))]
    cut = clen // 8
    top = to_next(states[:cut])

    rows = enc_rows.shape[1]
    block = width // parts
    columns = column_blocks(ids, enc_rows.reshape(rows, width), parts)
    columns = [columns[0]] + [flip(columns[r], r) for r in range(1, parts)]
    columns, w_query = barrier((columns, w_query))
    tiles = tile_mask.shape[2]
    flags = tile_mask.reshape(1, tiles, 1).astype(bf16)
    flags = jnp.broadcast_to(flags, (FLAG_ROWS, tiles, block // tiles)).reshape(FLAG_ROWS, block)
    piece = jnp.concatenate(columns + [flags], axis=0)
    piece, top = barrier((piece, top))
    gathered = lax.all_gather(piece, "cand", axis=0)
    states = jnp.concatenate([top, to_next(states[cut:])], axis=0)
    pairs.append((states, to_sib(states)))
    for hop in range(2, chips):
        states = to_next(states)
        pairs.append((states, to_sib(states)))

    near = near_blocks(w_query)
    query_parts = [w_query] + near + far_blocks(w_query, near)

    middle = block // 2
    left, right = w_out[:, :middle], w_out[:, middle:]
    near, left, early = barrier((near, left, right))
    out_near = [flip(left, 1), flip(early, 2)] if parts == 4 else []

    is_open, *sums = key_value(gathered, w_key, w_value, parts, rows, tiles)
    sums, out_near = barrier((sums, out_near))
    kv = sums[0]
    for r in range(1, parts):
        kv = kv + flip(sums[r], r).astype(f32)
    kv = kv.astype(bf16)
    if parts == 4:
        kv, left, right = barrier((kv, left, right))
        out_late = [flip(right, 1), flip(left, 2)]
        corner = [flip(out_near[0], 2), flip(out_near[1], 1)]
        out_chunks = [[w_out] + out_near, out_late + corner]
        places = [
            [(0, 0, block), (1, 0, middle), (2, middle, middle)],
            [(1, middle, middle), (2, 0, middle), (3, 0, middle), (3, middle, middle)],
        ]
    else:
        out_parts = [w_out] + [flip(w_out, r) for r in range(1, parts)]
        out_chunks = [out_parts[: parts // 2], out_parts[parts // 2 :]]
        places = [[(r, 0, block) for r in range(parts // 2)]]
        places += [[(r, 0, block) for r in range(parts // 2, parts)]]

    steps = list(range(1, chips)) + [0]
    passed = [None] * len(out_chunks)
    queries = [query(ids, *pairs[step], query_parts, parts) for step in steps]
    for index, step in enumerate(steps):
        context = attend(order, step, ids, queries[index], is_open, kv)
        last, totals = [], []
        for chunk, weights in enumerate(out_chunks):
            if index == 1 and chunk:
                context, passed[0] = barrier((context, passed[0]))
            mine, sib = project(context, weights)
            other = to_sib(sib)
            last += [mine, other, passed[chunk]]
            total = mine.astype(f32) + other.astype(f32)
            if index:
                total = total + passed[chunk].astype(f32)
            totals.append(total.astype(bf16))
        if not index:
            totals[0], queries[1] = barrier((totals[0], queries[1]))
        if step:
            passed = [to_next(total) for total in totals]
    return finish(places, ids, counts, last, parts, width).reshape(cand_states.shape)


def solution(mesh):
    parts, devices = mesh.shape["prod"], mesh.shape["cand"]
    return jax.shard_map(
        functools.partial(shards, parts, devices),
        mesh=mesh,
        in_specs=(
            P("prod", "cand", None, None),
            P("prod", "cand", None),
            P("prod", "cand"),
            P("prod", "cand"),
            P("prod", "cand"),
            P("cand", "prod"),
            P("prod", "cand", None),
            P("prod"),
        ),
        out_specs=P("prod", "cand", None, None),
        check_vma=False,
    )
```

```python
import functools

import jax
import jax.numpy as jnp
from jax import lax
from jax.experimental import pallas as pl
from jax.experimental.pallas import tpu as pltpu
from jax.sharding import PartitionSpec as P

HD = 64
TILE = 128
LANES = 128
FLAG_ROWS = 16
VMEM = pltpu.CompilerParams(vmem_limit_bytes=40 * 1024 * 1024)


def ring_order(chips):
    odd = list(range(1, chips, 2))
    even = list(range(2, chips, 2))
    return [0] + odd + even[::-1]


def small(flops=1):
    return pl.CostEstimate(flops=flops, bytes_accessed=1, transcendentals=0)


def columns_kernel(ids, x_ref, *outs):
    block = outs[0].shape[1]
    for r, out in enumerate(outs):
        source = jnp.bitwise_xor(ids[0], r)
        out[...] = x_ref[:, pl.ds(pl.multiple_of(source * block, block), block)]


def column_blocks(ids, x, parts):
    shape = jax.ShapeDtypeStruct((x.shape[0], x.shape[1] // parts), x.dtype)
    return pl.pallas_call(
        columns_kernel,
        out_shape=[shape] * parts,
        in_specs=[
            pl.BlockSpec(memory_space=pltpu.SMEM),
            pl.BlockSpec(memory_space=pltpu.VMEM),
        ],
        out_specs=[pl.BlockSpec(memory_space=pltpu.VMEM)] * parts,
        compiler_params=VMEM,
        cost_estimate=small(),
        name="columns",
    )(ids, x)


def key_value_kernel(parts, rows, tiles, enc_ref, w_key, w_value, open_ref, *outs):
    slots, height, block = enc_ref.shape
    local = w_key.shape[1]
    elen = slots * rows
    encoder = jnp.concatenate([enc_ref[slot, : parts * rows, :] for slot in range(slots)], axis=0)
    for column, weight in ((0, w_key), (local, w_value)):
        sums = jnp.dot(encoder, weight[...], preferred_element_type=jnp.float32)
        for r, out in enumerate(outs):
            for slot in range(slots):
                start, target = (slot * parts + r) * rows, slot * rows
                out[target : target + rows, column : column + local] = sums[
                    start : start + rows
                ].astype(out.dtype)
    tile = lax.broadcasted_iota(jnp.int32, (1, elen), 1) // TILE
    for slot in range(slots):
        seen = jnp.zeros((1, elen), jnp.float32)
        for t in range(tiles):
            start = t * (block // tiles)
            flag = enc_ref[slot, height - 1 : height, start : start + elen].astype(jnp.float32)
            seen = jnp.where(tile == t, flag, seen)
        open_ref[slot : slot + 1, :] = seen


def key_value(gathered, w_key, w_value, parts, rows, tiles):
    slots, local = gathered.shape[0], w_key.shape[1]
    elen = slots * rows
    return pl.pallas_call(
        functools.partial(key_value_kernel, parts, rows, tiles),
        out_shape=[jax.ShapeDtypeStruct((slots, elen), jnp.float32)]
        + [
            jax.ShapeDtypeStruct((elen, 2 * local), jnp.bfloat16 if r else jnp.float32)
            for r in range(parts)
        ],
        in_specs=[pl.BlockSpec(memory_space=pltpu.VMEM)] * 3,
        out_specs=[pl.BlockSpec(memory_space=pltpu.VMEM)] * (parts + 1),
        compiler_params=pltpu.CompilerParams(vmem_limit_bytes=58 * 1024 * 1024),
        cost_estimate=small(3 * 10**9),
        name="key_value",
    )(gathered, w_key, w_value)


def query_kernel(pieces, parts, ids, mine, sib, *refs):
    weights, out_ref = refs[:pieces], refs[pieces]
    clen, width = mine.shape
    block = width // parts
    scales = []
    for ref in (mine, sib):
        values = ref[...].astype(jnp.float32)
        scales.append(lax.rsqrt(jnp.sum(values * values, axis=-1, keepdims=True) / width + 1e-06))
    total, start = None, 0
    for weight in weights:
        depth = weight.shape[0]
        from_prod = jnp.bitwise_xor(ids[0], start // block)
        source = pl.multiple_of(from_prod * block + start % block, LANES)
        rows = jnp.concatenate(
            [
                (ref[:, pl.ds(source, depth)].astype(jnp.float32) * scale).astype(jnp.bfloat16)
                for ref, scale in zip((mine, sib), scales)
            ],
            axis=0,
        )
        term = jnp.dot(rows, weight[...], preferred_element_type=jnp.float32)
        total = term if total is None else total + term
        start += depth
    out_ref[...] = total.astype(jnp.bfloat16)


def query(ids, mine, sib, weights, parts):
    clen = mine.shape[0]
    return pl.pallas_call(
        functools.partial(query_kernel, len(weights), parts),
        out_shape=jax.ShapeDtypeStruct((2 * clen, weights[0].shape[1]), jnp.bfloat16),
        in_specs=[pl.BlockSpec(memory_space=pltpu.SMEM)]
        + [pl.BlockSpec(memory_space=pltpu.VMEM)] * (2 + len(weights)),
        out_specs=pl.BlockSpec(memory_space=pltpu.VMEM),
        compiler_params=VMEM,
        cost_estimate=small(),
        name="query",
    )(ids, mine, sib, *weights)


def attend_kernel(order, step, ids, query_ref, open_ref, kv_ref, out_ref):
    chips = len(order)
    chip, core = lax.div(ids[1], 2), lax.rem(ids[1], 2)
    source = chip
    if step:
        for place in range(chips):
            source = jnp.where(chip == order[place], order[(place - step) % chips], source)
    who = (2 * source + core, 2 * source + 1 - core)
    clen = query_ref.shape[0] // 2
    elen, local = kv_ref.shape[0], kv_ref.shape[1] // 2
    is_open = (
        jnp.concatenate(
            [jnp.broadcast_to(open_ref[pl.ds(who[i], 1), :], (clen, elen)) for i in range(2)],
            axis=0,
        )
        > 0.5
    )
    lane = lax.broadcasted_iota(jnp.int32, (elen, LANES), 1) // HD
    for pair in range(local // LANES):
        columns = slice(pair * LANES, (pair + 1) * LANES)
        keys = kv_ref[:, columns]
        values = kv_ref[:, local + pair * LANES : local + (pair + 1) * LANES]
        context = None
        for half in range(LANES // HD):
            own = lane == half
            scores = (
                lax.dot_general(
                    query_ref[:, columns],
                    jnp.where(own, keys, jnp.zeros_like(keys)),
                    (((1,), (1,)), ((), ())),
                    preferred_element_type=jnp.float32,
                )
                * 0.125
            )
            scores = jnp.where(is_open, scores, -1e30)
            top = jnp.max(scores, axis=-1, keepdims=True)
            grown = jnp.exp(scores - top)
            probs = (grown / jnp.sum(grown, axis=-1, keepdims=True)).astype(jnp.bfloat16)
            term = jnp.dot(
                probs,
                jnp.where(own, values, jnp.zeros_like(values)),
                preferred_element_type=jnp.float32,
            )
            context = term if context is None else context + term
        out_ref[:, columns] = context.astype(jnp.bfloat16)


def attend(order, step, ids, queries, is_open, kv):
    return pl.pallas_call(
        functools.partial(attend_kernel, order, step),
        out_shape=jax.ShapeDtypeStruct(queries.shape, jnp.bfloat16),
        in_specs=[pl.BlockSpec(memory_space=pltpu.SMEM)]
        + [pl.BlockSpec(memory_space=pltpu.VMEM)] * 3,
        out_specs=pl.BlockSpec(memory_space=pltpu.VMEM),
        compiler_params=VMEM,
        cost_estimate=small(),
        name="attend",
    )(ids, queries, is_open, kv)


def project_kernel(pieces, context_ref, *refs):
    weights, (mine, sib) = refs[: len(pieces)], refs[len(pieces) :]
    clen = mine.shape[0]
    totals = {}
    for (r, row), weight in zip(pieces, weights):
        term = jnp.dot(
            context_ref[:, row : row + weight.shape[0]],
            weight[...],
            preferred_element_type=jnp.float32,
        )
        totals[r] = term if r not in totals else totals[r] + term
        if row + weight.shape[0] == context_ref.shape[1]:
            block = weight.shape[1]
            rows = totals[r].astype(jnp.bfloat16)
            mine[:, r * block : (r + 1) * block] = rows[:clen]
            sib[:, r * block : (r + 1) * block] = rows[clen:]


def project(context, weights):
    rows, local = context.shape
    pieces, row = [], 0
    for weight in weights:
        pieces.append((row // local, row % local))
        row += weight.shape[0]
    width = row // local * weights[0].shape[1]
    shape = jax.ShapeDtypeStruct((rows // 2, width), jnp.bfloat16)
    return pl.pallas_call(
        functools.partial(project_kernel, pieces),
        out_shape=[shape, shape],
        in_specs=[pl.BlockSpec(memory_space=pltpu.VMEM)] * (1 + len(weights)),
        out_specs=[pl.BlockSpec(memory_space=pltpu.VMEM)] * 2,
        compiler_params=VMEM,
        cost_estimate=small(),
        name="project",
    )(context, *weights)


def finish_kernel(parts, ids, counts, *refs):
    out_ref = refs[-1]
    chunks = (len(refs) - 1) // 3
    block = out_ref.shape[1] // parts
    live = jnp.where(ids[1] < counts[0], 1.0, 0.0)
    r = 0
    for chunk in range(chunks):
        mine, other, passed = refs[3 * chunk : 3 * chunk + 3]
        for start in range(0, mine.shape[1], block):
            columns = slice(start, start + block)
            total = mine[:, columns].astype(jnp.float32) + other[:, columns].astype(jnp.float32)
            total = total + passed[:, columns].astype(jnp.float32)
            target = pl.multiple_of(jnp.bitwise_xor(ids[0], r) * block, block)
            out_ref[:, pl.ds(target, block)] = (total * live).astype(jnp.bfloat16)
            r += 1


def finish(ids, counts, sums, parts, width):
    return pl.pallas_call(
        functools.partial(finish_kernel, parts),
        out_shape=jax.ShapeDtypeStruct((sums[0].shape[0], width), jnp.bfloat16),
        in_specs=[pl.BlockSpec(memory_space=pltpu.SMEM)] * 2
        + [pl.BlockSpec(memory_space=pltpu.VMEM)] * len(sums),
        out_specs=pl.BlockSpec(memory_space=pltpu.VMEM),
        compiler_params=VMEM,
        cost_estimate=small(),
        name="finish",
    )(ids, counts, *sums)


def shards(parts, devices, cand_states, enc_rows, w_query, w_key, w_value, w_out, tile_mask, counts):
    chips = devices // 2
    order = ring_order(chips)
    along = [
        (2 * order[i] + core, 2 * order[(i + 1) % chips] + core)
        for i in range(chips)
        for core in range(2)
    ]
    across = [(c, c ^ 1) for c in range(devices)]

    def to_next(value):
        return lax.ppermute(value, "cand", along)

    def to_sib(value):
        return lax.ppermute(value, "cand", across)

    def flip(value, r):
        return lax.ppermute(value, "prod", [(q, q ^ r) for q in range(parts)])

    ids = jnp.stack([lax.axis_index("prod"), lax.axis_index("cand")]).astype(jnp.int32)

    barrier = lax.optimization_barrier
    f32, bf16 = jnp.float32, jnp.bfloat16

    def near_blocks(weight):
        return [flip(weight, r) for r in range(1, min(parts, 3))]

    def far_blocks(weight, near):
        if parts != 4:
            return [flip(weight, r) for r in range(3, parts)]
        half = weight.shape[0] // 2
        return [flip(near[0][:half], 2), flip(near[1][half:], 1)]

    clen, width = cand_states.shape[2:]
    states = cand_states.reshape(clen, width)
    pairs = [(states, to_sib(states))]
    cut = clen // 8
    top = to_next(states[:cut])

    rows = enc_rows.shape[1]
    block = width // parts
    columns = column_blocks(ids, enc_rows.reshape(rows, width), parts)
    columns = [columns[0]] + [flip(columns[r], r) for r in range(1, parts)]
    columns, w_query = barrier((columns, w_query))
    tiles = tile_mask.shape[2]
    flags = tile_mask.reshape(1, tiles, 1).astype(bf16)
    flags = jnp.broadcast_to(flags, (FLAG_ROWS, tiles, block // tiles)).reshape(FLAG_ROWS, block)
    piece = jnp.concatenate(columns + [flags], axis=0)
    piece, top = barrier((piece, top))
    gathered = lax.all_gather(piece, "cand", axis=0)
    states = jnp.concatenate([top, to_next(states[cut:])], axis=0)
    pairs.append((states, to_sib(states)))
    for hop in range(2, chips):
        states = to_next(states)
        pairs.append((states, to_sib(states)))

    near = near_blocks(w_query)
    query_parts = [w_query] + near + far_blocks(w_query, near)
    near, w_out = barrier((near, w_out))
    out_near = near_blocks(w_out)

    is_open, *sums = key_value(gathered, w_key, w_value, parts, rows, tiles)
    sums, out_near = barrier((sums, out_near))
    out_parts = [w_out] + out_near + far_blocks(w_out, out_near)
    out_chunks = [out_parts[: parts // 2], out_parts[parts // 2 :]]
    kv = sums[0]
    for r in range(1, parts):
        kv = kv + flip(sums[r], r).astype(f32)
    kv = kv.astype(bf16)

    steps = list(range(1, chips)) + [0]
    passed = [None] * len(out_chunks)
    queries = [query(ids, *pairs[step], query_parts, parts) for step in steps]
    for index, step in enumerate(steps):
        context = attend(order, step, ids, queries[index], is_open, kv)
        last, totals = [], []
        for chunk, weights in enumerate(out_chunks):
            if index == 1 and not chunk:
                context, passed[0] = barrier((context, passed[0]))
            mine, sib = project(context, weights)
            other = to_sib(sib)
            last += [mine, other, passed[chunk]]
            total = mine.astype(f32) + other.astype(f32)
            if index:
                total = total + passed[chunk].astype(f32)
            totals.append(total.astype(bf16))
            if not index and not chunk:
                context, totals[0] = barrier((context, totals[0]))
        if step:
            passed = [to_next(total) for total in totals]
    return finish(ids, counts, last, parts, width).reshape(cand_states.shape)


def solution(mesh):
    parts, devices = mesh.shape["prod"], mesh.shape["cand"]
    return jax.shard_map(
        functools.partial(shards, parts, devices),
        mesh=mesh,
        in_specs=(
            P("prod", "cand", None, None),
            P("prod", "cand", None),
            P("prod", "cand"),
            P("prod", "cand"),
            P("prod", "cand"),
            P("cand", "prod"),
            P("prod", "cand", None),
            P("prod"),
        ),
        out_specs=P("prod", "cand", None, None),
        check_vma=False,
    )
```
